128 devices in a mesh: brow: 8 (over z, core), bcol: 16 (over x, y).
Axes of the slice: x: 4, y: 4, z: 4, core: 2. Of those that a mesh axis runs over, the one named last changes fastest.
Arguments:
- blocks: bfloat16 [8, 16, 40, 256, 256], P('brow', 'bcol'), may hold values from -6 to 6
- pattern_rows: int32 [8, 16, 40], P('brow', 'bcol'), may hold values from 0 to 47
- pattern_cols: int32 [8, 16, 40], P('brow', 'bcol'), may hold values from 0 to 23
- live_count: int32 [8, 16], P('brow', 'bcol'), may hold values from 10 to 40, as said below
- degree_scale: float32 [98304], P(('brow', 'bcol')), may hold values from 0.03125 to 0.125
- eigen_block: float32 [32, 98304], P(None, ('brow', 'bcol')), may hold values from -6 to 6
- direction: float32 [32, 98304], P(None, ('brow', 'bcol')), may hold values from -6 to 6
- cutoff: float32 [1], replicated, may hold values from 0.9 to 1
Outputs:
- eigen_next: float32 [32, 98304], P(None, ('brow', 'bcol'))
- direction_next: float32 [32, 98304], P(None, ('brow', 'bcol'))
- residual: float32 [32, 98304], P(None, ('brow', 'bcol'))
- direction_image: float32 [32, 98304], P(None, ('brow', 'bcol'))
The draws below stay inside these ranges and needn't reach their ends.
Inputs may be any that keep to these rules, and one draw needn't show every extreme that they name: `live_count`: some owner uses all 40 slots in every draw.
All inputs are finite; a program needn't handle non-finite values.
Results may differ from the reference program's by a relative error of at most 0.033.
Values may be sent and summed in bfloat16 or wider, within the bound.
No kernel may reach another device: no remote copies, remote signals or barrier semaphores. Data moves between devices by JAX's collectives and lax.ppermute only.
A program may use at most 64 MiB of HBM per device.

```python
import math
import jax
import jax.numpy as jnp
from jax import lax

BS = 256
K = 32
PIECE = 3
ITERS = 2
NS_STEPS = 8
SLOTS = 40
BROWS_LOC = 48
BCOLS_LOC = 24
DOCS = 98304
N_BROW = 8
N_BCOL = 16


def draw_live_count(key, part):
    key = jax.random.fold_in(key, 11)
    first_key, second_key, third_key = jax.random.split(key, 3)
    spread = SLOTS - SLOTS // 4
    owners = N_BROW * N_BCOL
    left_part = jax.random.randint(first_key, (owners,), 0, spread + 1)
    right_part = jax.random.randint(second_key, (owners,), 0, spread + 1)
    counts = SLOTS // 4 + left_part * right_part // spread
    busiest = jax.random.randint(third_key, (), 0, owners)
    counts = jnp.where(jnp.arange(owners) == busiest, SLOTS, counts)
    return counts.reshape(N_BROW, N_BCOL).astype(jnp.int32)


def with_ends(entries, stream_key, low, top_value):
    longest = entries.shape.index(max(entries.shape))
    spots = []
    for shift in (0, 1):
        where = [jax.random.randint(jax.random.fold_in(stream_key, axis), (), 0, length) for axis, length in enumerate(entries.shape)]
        where[longest] = (where[longest] + shift) % entries.shape[longest]
        spots.append(tuple(where))
    return entries.at[spots[0]].set(low).at[spots[1]].set(top_value)


def block_levels(key, extent, cuts, low, high):
    gain = 1.0
    for dim, parts in cuts:
        draws = jax.random.uniform(jax.random.fold_in(jax.random.fold_in(key, 6), dim), (parts,), jnp.float32, low / len(cuts), high / len(cuts))
        gain = gain * jnp.repeat(jnp.exp(draws), extent[dim] // parts).reshape((-1,) + (1,) * (len(extent) - 1 - dim))
    return gain


def noise(own_key, extent, width, most, cuts=(), held_as=jnp.bfloat16):
    factor_of = block_levels(own_key, extent, cuts, -0.22, 0.18) if cuts else 1.0
    values = jax.random.normal(own_key, extent, jnp.float32) * width * factor_of
    return jnp.minimum(jnp.maximum(values, -most), most).astype(held_as)


def setup_inputs(seed: int = 0) -> dict:
    arg_keys = jax.random.split(jax.random.key(seed), 9)
    return {
        "blocks": noise(arg_keys[0], (N_BROW, N_BCOL, SLOTS, BS, BS), 1.0, 6.0, ((0, 8), (1, 16))),
        "pattern_rows": with_ends(jax.random.randint(arg_keys[1], (N_BROW, N_BCOL, SLOTS), 0, BROWS_LOC), jax.random.fold_in(arg_keys[1], 1), 0, BROWS_LOC - 1).astype(jnp.int32),
        "pattern_cols": with_ends(jax.random.randint(arg_keys[2], (N_BROW, N_BCOL, SLOTS), 0, BCOLS_LOC), jax.random.fold_in(arg_keys[2], 1), 0, BCOLS_LOC - 1).astype(jnp.int32),
        "live_count": draw_live_count(jax.random.fold_in(arg_keys[8], 71), 0),
        "degree_scale": jnp.clip(jnp.exp(math.log(0.125) - 1.3862944 * jax.random.uniform(arg_keys[4], (DOCS,), jnp.float32) ** block_levels(arg_keys[4], (DOCS,), ((0, 128),), -0.2, 0.2)), 0.03125, 0.125),
        "eigen_block": noise(arg_keys[5], (K, DOCS), 1.0, 6.0, ((1, 128),), jnp.float32),
        "direction": noise(arg_keys[6], (K, DOCS), 1.0, 6.0, ((1, 128),), jnp.float32),
        "cutoff": jnp.clip(jax.random.uniform(arg_keys[7], (1,), jnp.float32, 0.9, 1.0), 0.9, 1.0),
    }


def graph_product(blocks, pattern_rows, pattern_cols, live_count, stack_rows):
    columns = stack_rows.shape[0]
    pieces = stack_rows.reshape(columns, N_BROW, N_BCOL, PIECE * BS)
    slot_index = jnp.arange(SLOTS)

    def per_owner(row_owner):

        def per_column(total, col_owner):
            panel = jnp.take(pieces, col_owner, axis=2).reshape(columns, N_BROW * PIECE, BS)
            picked = jnp.take(panel, pattern_cols[row_owner, col_owner], axis=1).astype(jnp.float32)
            products = jnp.einsum('sab,csb->csa', blocks[row_owner, col_owner].astype(jnp.float32), picked)
            kept_mask = (slot_index < live_count[row_owner, col_owner]).astype(jnp.float32)
            partial_value = jnp.zeros((columns, N_BCOL * PIECE, BS), jnp.float32)
            partial_value = partial_value.at[:, pattern_rows[row_owner, col_owner]].add(products * kept_mask[None, :, None])
            partial_value = lax.optimization_barrier(partial_value.astype(jnp.bfloat16)).astype(jnp.float32)
            return (total + partial_value.reshape(columns, -1), None)
        start_sum = jnp.zeros((columns, N_BCOL * PIECE * BS), jnp.float32)
        total, _ = lax.scan(per_column, start_sum, jnp.arange(N_BCOL))
        return total
    owners = lax.map(per_owner, jnp.arange(N_BROW))
    return jnp.transpose(owners, (1, 0, 2)).reshape(columns, -1)

def highest_dot(left, right):
    return jnp.dot(left, right, precision=lax.Precision.HIGHEST)

def solve_quotient(gram_x, rayleigh_x):
    lower = jnp.linalg.cholesky(gram_x)
    middle = lax.linalg.triangular_solve(lower, rayleigh_x, left_side=True, lower=True)
    return lax.linalg.triangular_solve(lower, middle, left_side=True, lower=True, transpose_a=True)

def ritz_coefficients(gram_b, gram_a, cutoff, wanted):
    lower = jnp.linalg.cholesky(gram_b)
    first = lax.linalg.triangular_solve(lower, gram_a, left_side=True, lower=True)
    small = lax.linalg.triangular_solve(lower, first.T, left_side=True, lower=True)
    identity = jnp.eye(small.shape[0], dtype=jnp.float32)
    shifted = cutoff[0] * identity - small
    sign_now = shifted / jnp.sqrt(jnp.sum(shifted * shifted) + 1e-06)
    for sweep_index in range(NS_STEPS):
        sign_now = 1.5 * sign_now - 0.5 * highest_dot(sign_now, highest_dot(sign_now, sign_now))
    projector = 0.5 * (identity + sign_now)
    inner = highest_dot(projector, lower.T[:, :wanted])
    return lax.linalg.triangular_solve(lower, inner, left_side=True, lower=True, transpose_a=True)

def reference(blocks, pattern_rows, pattern_cols, live_count, degree_scale, eigen_block, direction, cutoff):
    wanted = eigen_block.shape[0]
    vectors, searches = (eigen_block, direction)
    for section_index in range(ITERS + 1):
        panel = (degree_scale * jnp.concatenate([vectors, searches], 0)).astype(jnp.bfloat16)
        image = graph_product(blocks, pattern_rows, pattern_cols, live_count, panel)
        image_x = vectors - degree_scale * image[:wanted]
        image_p = searches - degree_scale * image[wanted:]
        gram_x = highest_dot(vectors, vectors.T)
        rayleigh_x = highest_dot(vectors, image_x.T)
        quotient = solve_quotient(gram_x, rayleigh_x)
        remainder = image_x - highest_dot(quotient.T, vectors)
        if section_index < ITERS:
            residual_panel = (degree_scale * remainder).astype(jnp.bfloat16)
            image_r = remainder - degree_scale * graph_product(blocks, pattern_rows, pattern_cols, live_count, residual_panel)
            basis = jnp.concatenate([vectors, remainder, searches], 0)
            basis_image = jnp.concatenate([image_x, image_r, image_p], 0)
            gram_b = highest_dot(basis, basis.T)
            cross = highest_dot(basis, basis_image.T)
            gram_a = 0.5 * (cross + cross.T)
            coeffs = ritz_coefficients(gram_b, gram_a, cutoff, wanted)
            row_mask = (jnp.arange(coeffs.shape[0]) >= wanted).astype(jnp.float32)
            vectors_new = highest_dot(coeffs.T, basis)
            searches = highest_dot((coeffs * row_mask[:, None]).T, basis)
            vectors = vectors_new
    return (vectors, searches, remainder, image_p)
```

```python
import functools

import jax
import jax.numpy as jnp
from jax import lax
from jax.experimental import pallas as pl
from jax.experimental.pallas import tpu as pltpu
from jax.sharding import PartitionSpec as P

ITERS = 2
NS_STEPS = 8
CHUNK = 8
HIGH = lax.Precision.HIGHEST
BF = jnp.bfloat16
F32 = jnp.float32


def nn(a, b):
    return lax.dot_general(a, b, (((1,), (0,)), ((), ())), precision=HIGH, preferred_element_type=F32)


def nt(a, b):
    return lax.dot_general(a, b, (((1,), (1,)), ((), ())), precision=HIGH, preferred_element_type=F32)


def graph_kernel(n_slots, live_ref, rows_ref, cols_ref, near_ref, far_ref, blocks_ref, out_ref,
                 held, panel, acc, sems):
    chunks = n_slots // CHUNK
    live = live_ref[0]

    def fetch(c):
        part = pl.ds(c * CHUNK, CHUNK)
        return pltpu.make_async_copy(blocks_ref.at[part], held.at[part], sems.at[c])

    for c in range(chunks):
        @pl.when(c * CHUNK < live)
        def _():
            fetch(c).start()
    sub = panel.shape[0] // 8
    for s in range(8):
        src = near_ref if s < 4 else far_ref
        for q in range(sub):
            panel[s * sub + q] = src[s % 4, :, q * 256:(q + 1) * 256]
    acc[...] = jnp.zeros_like(acc)
    for c in range(chunks):
        @pl.when(c * CHUNK < live)
        def _():
            fetch(c).wait()
            for t in range(CHUNK):
                s = c * CHUNK + t
                prod = lax.dot_general(panel[cols_ref[s]], held[s], (((1,), (1,)), ((), ())),
                                       preferred_element_type=F32)
                row = rows_ref[s]
                acc[row] = acc[row] + prod
    for j in range(out_ref.shape[0]):
        for q in range(sub):
            out_ref[j, :, q * 256:(q + 1) * 256] = acc[j * sub + q].astype(BF)


def graph_partial(live, rows, cols, near, far, blocks, owners):
    n_slots, side, _ = blocks.shape
    r, width = near.shape[1:]
    sub = width // side
    return pl.pallas_call(
        functools.partial(graph_kernel, n_slots),
        out_shape=jax.ShapeDtypeStruct((owners, r, width), BF),
        in_specs=[pl.BlockSpec(memory_space=pltpu.SMEM)] * 3
        + [pl.BlockSpec(memory_space=pltpu.VMEM)] * 2
        + [pl.BlockSpec(memory_space=pl.ANY)],
        out_specs=pl.BlockSpec(memory_space=pltpu.VMEM),
        scratch_shapes=[
            pltpu.VMEM((n_slots, side, side), BF),
            pltpu.VMEM((8 * sub, r, side), BF),
            pltpu.VMEM((owners * sub + 1, r, side), F32),
            pltpu.SemaphoreType.DMA((n_slots // CHUNK,)),
        ],
        compiler_params=pltpu.CompilerParams(vmem_limit_bytes=32 * 2**20),
        name="graph_partial",
    )(live, rows, cols, near, far, blocks)


def spd_inverse(a):
    n = a.shape[0]
    ri = lax.broadcasted_iota(jnp.int32, (n, n), 0)
    ci = lax.broadcasted_iota(jnp.int32, (n, n), 1)
    r1 = lax.broadcasted_iota(jnp.int32, (n, 1), 0)
    c1 = lax.broadcasted_iota(jnp.int32, (1, n), 1)
    for k in range(n):
        p = 1.0 / a[k:k + 1, k:k + 1]
        row = jnp.where(c1 == k, -1.0, a[k:k + 1, :]) * p
        col = jnp.where(r1 == k, -1.0, a[:, k:k + 1])
        a = jnp.where((ri == k) | (ci == k), 0.0, a) - col * row
    return -a


def residual_coeffs(x, h, shift):
    tx = nn(x, h)
    gram = nt(tx, x)
    moved = shift(x)
    zt = nn(nt(moved, tx), spd_inverse(gram))
    return nn(zt, x) - moved


def ritz_rows(basis, h, cutoff, shift, wanted):
    tb = nn(basis, h)
    moved = shift(basis)
    gram = nt(tb, basis)
    sym = 0.5 * (nt(tb, moved) + nt(moved, tb))
    n = gram.shape[0]
    eye = (lax.broadcasted_iota(jnp.int32, (n, n), 0)
           == lax.broadcasted_iota(jnp.int32, (n, n), 1)).astype(F32)
    s = (cutoff - 1.0) * eye + nn(sym, spd_inverse(gram))
    s2 = nn(s, s)
    total = jnp.sum(jnp.sum(s2 * eye, axis=1, keepdims=True), axis=0, keepdims=True)
    scale = lax.rsqrt(total + 1e-06)
    s = s * scale
    s2 = s2 * (scale * scale)
    s = 1.5 * s - 0.5 * nn(s, s2)
    for _ in range(NS_STEPS - 1):
        s = 1.5 * s - 0.5 * nn(s, nn(s, s))
    return 0.5 * (eye + s)[:wanted]


def small_math(h, cutoff, wanted, shift):
    width = h.shape[0]
    ri = lax.broadcasted_iota(jnp.int32, (wanted, width), 0)
    ci = lax.broadcasted_iota(jnp.int32, (wanted, width), 1)
    x = (ri == ci).astype(F32)
    p = (ri + wanted == ci).astype(F32)
    for _ in range(ITERS):
        r = residual_coeffs(x, h, shift)
        basis = jnp.concatenate([x, r, p], 0)
        rows = ritz_rows(basis, h, cutoff, shift, wanted)
        keep = lax.broadcasted_iota(jnp.int32, rows.shape, 1) >= wanted
        both = nn(jnp.concatenate([rows, jnp.where(keep, rows, 0.0)], 0), basis)
        x, p = both[:wanted], both[wanted:]
    r = residual_coeffs(x, h, shift)
    return jnp.concatenate([x, p, r, p - shift(p)], 0)


def small_kernel(wanted, cut_ref, g_ref, out_ref):
    pieces, cols = g_ref.shape
    width = out_ref.shape[1]
    h = jnp.concatenate([g_ref[...], jnp.zeros((width - pieces, cols), F32)], 0)
    out_ref[...] = small_math(h, cut_ref[0], wanted, lambda v: pltpu.roll(v, 2 * wanted, 1))


def small(cutoff, gram, wanted):
    return pl.pallas_call(
        functools.partial(small_kernel, wanted),
        out_shape=jax.ShapeDtypeStruct((4 * wanted, gram.shape[1]), F32),
        in_specs=[pl.BlockSpec(memory_space=pltpu.SMEM), pl.BlockSpec(memory_space=pltpu.VMEM)],
        out_specs=pl.BlockSpec(memory_space=pltpu.VMEM),
        compiler_params=pltpu.CompilerParams(vmem_limit_bytes=32 * 2**20),
        name="small_matrices",
    )(cutoff, gram)


def z_turn(k):
    return [(i, (i + 2 * k) % 8) for i in range(8)]


def y_turn(k):
    return [(i, (i // 4) * 4 + (i + k) % 4) for i in range(16)]


def x_turn(k):
    return [(i, (i + 4 * k) % 16) for i in range(16)]


CORE = [(i, i ^ 1) for i in range(8)]


def gather_brow(v):
    near = jnp.stack([v] + [lax.ppermute(v, "brow", z_turn(k)) for k in (1, 2, 3)])
    return near, lax.ppermute(near, "brow", CORE)


def sum_all(g):
    half = g.shape[0] // 2
    me = lax.axis_index("brow") % 2
    mine = lax.dynamic_slice_in_dim(g, me * half, half, 0)
    other = lax.dynamic_slice_in_dim(g, (1 - me) * half, half, 0)
    v = mine + lax.ppermute(other, "brow", CORE)
    for axis, turn in (("brow", z_turn), ("bcol", y_turn), ("bcol", x_turn)):
        a, b, c = [lax.ppermute(v, axis, turn(k)) for k in (1, 2, 3)]
        v = (v + a) + (b + c)
    w = lax.ppermute(v, "brow", CORE)
    first = jnp.where(me == 0, v, w)
    second = jnp.where(me == 0, w, v)
    return jnp.concatenate([first, second], 0)


def local(blocks, pattern_rows, pattern_cols, live_count, degree_scale, eigen_block, direction, cutoff):
    block_set = blocks[0, 0]
    n_slots, side, _ = block_set.shape
    wanted, width = eigen_block.shape
    sub = width // side
    owners = lax.axis_size("bcol")
    live = live_count.reshape(1)
    brow = lax.axis_index("brow")
    rows = jnp.where(jnp.arange(n_slots) < live[0], pattern_rows[0, 0], owners * sub)
    col = pattern_cols[0, 0]
    src = col // sub
    cols = ((brow // 2 - src // 2) % 4 + 4 * ((brow - src) % 2)) * sub + col % sub

    def apply_graph(v):
        near, far = gather_brow((degree_scale * v).astype(BF))
        part = graph_partial(live, rows, cols, near, far, block_set, owners)
        got = lax.all_to_all(part, "bcol", 0, 0)
        return degree_scale * jnp.sum(got.astype(F32), axis=0)

    k0 = jnp.concatenate([eigen_block, direction], 0)
    k1 = apply_graph(k0)
    k2 = apply_graph(k1)
    k3 = apply_graph(k2[:wanted])
    krylov = jnp.concatenate([k0, k1, k2, k3, jnp.zeros((wanted, width), F32)], 0)
    gram = nt(krylov[:5 * wanted], krylov)
    gram = sum_all(gram)
    coeffs = small(cutoff, gram, wanted)
    out = nn(coeffs, krylov)
    return out[:wanted], out[wanted:2 * wanted], out[2 * wanted:3 * wanted], out[3 * wanted:]


def solution(mesh):
    docs = P(None, ("brow", "bcol"))
    return jax.shard_map(
        local,
        mesh=mesh,
        in_specs=(
            P("brow", "bcol", None, None, None),
            P("brow", "bcol", None),
            P("brow", "bcol", None),
            P("brow", "bcol"),
            P(("brow", "bcol")),
            docs,
            docs,
            P(),
        ),
        out_specs=(docs, docs, docs, docs),
        check_vma=False,
    )
```

```python
import functools

import jax
import jax.numpy as jnp
from jax import lax
from jax.experimental import pallas as pl
from jax.experimental.pallas import tpu as pltpu
from jax.sharding import PartitionSpec as P

ITERS = 2
NS_STEPS = 8
CHUNK = 8
HIGH = lax.Precision.HIGHEST
BF = jnp.bfloat16
F32 = jnp.float32


def nn(a, b):
    return lax.dot_general(a, b, (((1,), (0,)), ((), ())), precision=HIGH, preferred_element_type=F32)


def nt(a, b):
    return lax.dot_general(a, b, (((1,), (1,)), ((), ())), precision=HIGH, preferred_element_type=F32)


def graph_kernel(n_slots, live_ref, rows_ref, cols_ref, near_ref, far_ref, blocks_ref, out_ref,
                 held, panel, acc, sems):
    chunks = n_slots // CHUNK
    live = live_ref[0]

    def fetch(c):
        part = pl.ds(c * CHUNK, CHUNK)
        return pltpu.make_async_copy(blocks_ref.at[part], held.at[part], sems.at[c])

    for c in range(chunks):
        @pl.when(c * CHUNK < live)
        def _():
            fetch(c).start()
    sub = panel.shape[0] // 8
    for s in range(8):
        src = near_ref if s < 4 else far_ref
        for q in range(sub):
            panel[s * sub + q] = src[s % 4, :, q * 256:(q + 1) * 256]
    acc[...] = jnp.zeros_like(acc)
    for c in range(chunks):
        @pl.when(c * CHUNK < live)
        def _():
            fetch(c).wait()
            for t in range(CHUNK):
                s = c * CHUNK + t
                prod = lax.dot_general(panel[cols_ref[s]], held[s], (((1,), (1,)), ((), ())),
                                       preferred_element_type=F32)
                row = rows_ref[s]
                acc[row] = acc[row] + prod
    for j in range(out_ref.shape[0]):
        for q in range(sub):
            out_ref[j, :, q * 256:(q + 1) * 256] = acc[j * sub + q].astype(BF)


def graph_partial(live, rows, cols, near, far, blocks, owners):
    n_slots, side, _ = blocks.shape
    r, width = near.shape[1:]
    sub = width // side
    return pl.pallas_call(
        functools.partial(graph_kernel, n_slots),
        out_shape=jax.ShapeDtypeStruct((owners, r, width), BF),
        in_specs=[pl.BlockSpec(memory_space=pltpu.SMEM)] * 3
        + [pl.BlockSpec(memory_space=pltpu.VMEM)] * 2
        + [pl.BlockSpec(memory_space=pltpu.HBM)],
        out_specs=pl.BlockSpec(memory_space=pltpu.VMEM),
        scratch_shapes=[
            pltpu.VMEM((n_slots, side, side), BF),
            pltpu.VMEM((8 * sub, r, side), BF),
            pltpu.VMEM((owners * sub + 1, r, side), F32),
            pltpu.SemaphoreType.DMA((n_slots // CHUNK,)),
        ],
        compiler_params=pltpu.CompilerParams(vmem_limit_bytes=50 * 2**20),
        name="graph_partial",
    )(live, rows, cols, near, far, blocks)


def eye_mask(n):
    return (lax.broadcasted_iota(jnp.int32, (n, n), 0) == lax.broadcasted_iota(jnp.int32, (n, n), 1))


def sweep_inverse(ref):
    n = ref.shape[0]
    ri = lax.broadcasted_iota(jnp.int32, (n, n), 0)
    ci = lax.broadcasted_iota(jnp.int32, (n, n), 1)

    def step(k, carry):
        a = ref[...]
        col = jnp.sum(jnp.where(ci == k, a, 0.0), axis=1, keepdims=True)
        row = jnp.sum(jnp.where(ri == k, a, 0.0), axis=0, keepdims=True)
        pivot = jnp.sum(jnp.where(ci[:1] == k, row, 0.0), axis=1, keepdims=True)
        col = jnp.where(ri[:, :1] == k, -1.0, col)
        row = jnp.where(ci[:1] == k, -1.0, row) / pivot
        ref[...] = jnp.where((ri == k) | (ci == k), 0.0, a) - col * row
        return carry

    lax.fori_loop(0, n, step, 0)
    ref[...] = -ref[...]


def square_sum(a):
    return jnp.sum(a * a)


def spd_inverses(mats, refs):
    scaled, lefts, rights, errs, sums = [], [], [], [], []
    for a in mats:
        eye = eye_mask(a.shape[0])
        diag = jnp.where(eye, a, 0.0)
        left = lax.rsqrt(jnp.sum(diag, axis=1, keepdims=True))
        right = lax.rsqrt(jnp.sum(diag, axis=0, keepdims=True))
        a = a * left * right
        rows = jnp.sum(jnp.abs(a), axis=0, keepdims=True)
        inv = 1.0 / jnp.max(rows, axis=1, keepdims=True)
        unit = eye.astype(F32)
        err = unit - a * inv
        scaled.append(a)
        lefts.append(left)
        rights.append(right)
        errs.append(err)
        sums.append((unit + err) * inv)

    def levels(errs, sums, count):
        for _ in range(count):
            errs = [nn(e, e) for e in errs]
            sums = [s + nn(s, e) for s, e in zip(sums, errs)]
        for (err_ref, sum_ref), e, s in zip(refs, errs, sums):
            err_ref[...] = e
            sum_ref[...] = s
        return sum(square_sum(e) for e in errs)

    def body(state):
        level, _ = state
        size = levels([r[0][...] for r in refs], [r[1][...] for r in refs], 2)
        return level + 1, size

    size = levels(errs, sums, 4)
    _, size = lax.while_loop(lambda s: (s[1] > 1e-16) & (s[0] < 12), body, (jnp.int32(0), size))
    good = size <= 1e-16

    @pl.when(good)
    def _():
        for a, (_, sum_ref) in zip(scaled, refs):
            s = sum_ref[...]
            sum_ref[...] = 2.0 * s - nn(s, nn(a, s))

    @pl.when(jnp.logical_not(good))
    def _():
        for a, (_, sum_ref) in zip(scaled, refs):
            sum_ref[...] = a
            sweep_inverse(sum_ref)

    return [left * r[1][...] * right for left, right, r in zip(lefts, rights, refs)]


def sign_rows(sym, inverse, cutoff, wanted):
    eye = eye_mask(sym.shape[0]).astype(F32)
    s = (cutoff - 1.0) * eye + nn(sym, inverse)
    s2 = nn(s, s)
    total = jnp.sum(jnp.sum(s2 * eye, axis=1, keepdims=True), axis=0, keepdims=True)
    scale = lax.rsqrt(total + 1e-06)
    s = s * scale
    s2 = s2 * (scale * scale)
    s = 1.5 * s - 0.5 * nn(s, s2)
    for _ in range(NS_STEPS - 1):
        s = 1.5 * s - 0.5 * nn(s, nn(s, s))
    return 0.5 * (eye + s)[:wanted]


def small_math(h, cutoff, wanted, shift, refs):
    width = h.shape[0]
    ri = lax.broadcasted_iota(jnp.int32, (wanted, width), 0)
    ci = lax.broadcasted_iota(jnp.int32, (wanted, width), 1)
    x = (ri == ci).astype(F32)
    p = (ri + wanted == ci).astype(F32)
    for _ in range(ITERS):
        basis = jnp.concatenate([x, shift(x), p], 0)
        tb = nn(basis, h)
        moved = shift(basis)
        gram = nt(tb, basis)
        sym = 0.5 * (nt(tb, moved) + nt(moved, tb))
        inverse, inverse_x = spd_inverses([gram, gram[:wanted, :wanted]], refs)
        zt = nn(gram[wanted:2 * wanted, :wanted], inverse_x)
        rows = sign_rows(sym, inverse, cutoff, wanted)
        searched = nn(rows[:, wanted:2 * wanted], zt)
        x, p = nn(rows, basis), nn(jnp.concatenate([-searched, rows[:, wanted:]], 1), basis)
    tx = nn(x, h)
    moved = shift(x)
    (inverse_x,) = spd_inverses([nt(tx, x)], refs[1:])
    zt = nn(nt(moved, tx), inverse_x)
    r = nn(zt, x) - moved
    return jnp.concatenate([x, p, r, p - shift(p)], 0)


def small_kernel(wanted, cut_ref, g_ref, out_ref, e96, s96, e32, s32):
    pieces, cols = g_ref.shape
    width = out_ref.shape[1]
    h = jnp.concatenate([g_ref[...], jnp.zeros((width - pieces, cols), F32)], 0)
    out_ref[...] = small_math(h, cut_ref[0], wanted, lambda v: pltpu.roll(v, 2 * wanted, 1),
                              [(e96, s96), (e32, s32)])


def small(cutoff, gram, wanted):
    return pl.pallas_call(
        functools.partial(small_kernel, wanted),
        out_shape=jax.ShapeDtypeStruct((4 * wanted, gram.shape[1]), F32),
        in_specs=[pl.BlockSpec(memory_space=pltpu.SMEM), pl.BlockSpec(memory_space=pltpu.VMEM)],
        out_specs=pl.BlockSpec(memory_space=pltpu.VMEM),
        scratch_shapes=[pltpu.VMEM((n, n), F32) for n in (3 * wanted, 3 * wanted, wanted, wanted)],
        compiler_params=pltpu.CompilerParams(vmem_limit_bytes=16 * 2**20),
        name="small_matrices",
    )(cutoff, gram)


def z_turn(k):
    return [(i, (i + 2 * k) % 8) for i in range(8)]


def y_turn(k):
    return [(i, (i // 4) * 4 + (i + k) % 4) for i in range(16)]


def x_turn(k):
    return [(i, (i + 4 * k) % 16) for i in range(16)]


CORE = [(i, i ^ 1) for i in range(8)]


def gather_brow(v):
    near = jnp.stack([v] + [lax.ppermute(v, "brow", z_turn(k)) for k in (1, 2, 3)])
    return near, lax.ppermute(near, "brow", CORE)


def sum_all(g):
    half = g.shape[0] // 2
    me = lax.axis_index("brow") % 2
    mine = lax.dynamic_slice_in_dim(g, me * half, half, 0)
    other = lax.dynamic_slice_in_dim(g, (1 - me) * half, half, 0)
    v = mine + lax.ppermute(other, "brow", CORE)
    for axis, turn in (("brow", z_turn), ("bcol", y_turn), ("bcol", x_turn)):
        a, b, c = [lax.ppermute(v, axis, turn(k)) for k in (1, 2, 3)]
        v = (v + a) + (b + c)
    w = lax.ppermute(v, "brow", CORE)
    first = jnp.where(me == 0, v, w)
    second = jnp.where(me == 0, w, v)
    return jnp.concatenate([first, second], 0)


def local(blocks, pattern_rows, pattern_cols, live_count, degree_scale, eigen_block, direction, cutoff):
    block_set = blocks[0, 0]
    n_slots, side, _ = block_set.shape
    wanted, width = eigen_block.shape
    sub = width // side
    owners = lax.axis_size("bcol")
    live = live_count.reshape(1)
    brow = lax.axis_index("brow")
    rows = jnp.where(jnp.arange(n_slots) < live[0], pattern_rows[0, 0], owners * sub)
    col = pattern_cols[0, 0]
    src = col // sub
    cols = ((brow // 2 - src // 2) % 4 + 4 * ((brow - src) % 2)) * sub + col % sub

    def apply_graph(v):
        near, far = gather_brow((degree_scale * v).astype(BF))
        part = graph_partial(live, rows, cols, near, far, block_set, owners)
        got = lax.all_to_all(part, "bcol", 0, 0)
        return degree_scale * jnp.sum(got.astype(F32), axis=0)

    k0 = jnp.concatenate([eigen_block, direction], 0)
    k1 = apply_graph(k0)
    k2 = apply_graph(k1)
    k3 = apply_graph(k2[:wanted])
    krylov = jnp.concatenate([k0, k1, k2, k3, jnp.zeros((wanted, width), F32)], 0)
    gram = nt(krylov[:5 * wanted], krylov)
    gram = sum_all(gram)
    coeffs = small(cutoff, gram, wanted)
    out = nn(coeffs, krylov)
    return out[:wanted], out[wanted:2 * wanted], out[2 * wanted:3 * wanted], out[3 * wanted:]


def solution(mesh):
    docs = P(None, ("brow", "bcol"))
    return jax.shard_map(
        local,
        mesh=mesh,
        in_specs=(
            P("brow", "bcol", None, None, None),
            P("brow", "bcol", None),
            P("brow", "bcol", None),
            P("brow", "bcol"),
            P(("brow", "bcol")),
            docs,
            docs,
            P(),
        ),
        out_specs=(docs, docs, docs, docs),
        check_vma=False,
    )
```

```python
import functools

import jax
import jax.numpy as jnp
from jax import lax
from jax.experimental import pallas as pl
from jax.experimental.pallas import tpu as pltpu
from jax.sharding import PartitionSpec as P

ITERS = 2
NS_STEPS = 8
CHUNK = 8
HIGH = lax.Precision.HIGHEST
BF = jnp.bfloat16
F32 = jnp.float32
SMEM = pl.BlockSpec(memory_space=pltpu.SMEM)
VMEM = pl.BlockSpec(memory_space=pltpu.VMEM)


def nn(a, b):
    return lax.dot_general(a, b, (((1,), (0,)), ((), ())), precision=HIGH, preferred_element_type=F32)


def nt(a, b):
    return lax.dot_general(a, b, (((1,), (1,)), ((), ())), precision=HIGH, preferred_element_type=F32)


def graph_kernel(place_ref, rows_ref, cols_ref, near_ref, far_ref, blocks_ref, out_ref, panel, acc, *own):
    live, brow = place_ref[0], place_ref[1]
    n_slots = blocks_ref.shape[0]
    sub = panel.shape[0] // 8
    chunks = n_slots // CHUNK
    held = own[0] if own else blocks_ref

    def fetch(c):
        part = pl.ds(c * CHUNK, CHUNK)
        return pltpu.make_async_copy(blocks_ref.at[part], held.at[part], own[1].at[c])

    for c in range(chunks if own else 0):
        @pl.when(c * CHUNK < live)
        def _():
            fetch(c).start()

    for s in range(8):
        src = near_ref if s < 4 else far_ref
        for q in range(sub):
            panel[s * sub + q] = src[s % 4, :, q * 256:(q + 1) * 256]
    acc[...] = jnp.zeros_like(acc)

    def spot(slot):
        source = lax.div(cols_ref[slot], sub)
        turn = jnp.bitwise_and(lax.div(brow, 2) - lax.div(source, 2), 3)
        side = jnp.bitwise_and(brow - source, 1)
        return (turn + 4 * side) * sub + lax.rem(cols_ref[slot], sub)

    for c in range(chunks):
        @pl.when(c * CHUNK < live)
        def _():
            if own:
                fetch(c).wait()
            slots = range(c * CHUNK, (c + 1) * CHUNK)
            prods = [lax.dot_general(panel[spot(s)], held[s], (((1,), (1,)), ((), ())),
                                     preferred_element_type=F32) for s in slots]
            for s, prod in zip(slots, prods):
                row = jnp.where(s < live, rows_ref[s], acc.shape[0] - 1)
                acc[row] = acc[row] + prod
    for j in range(out_ref.shape[0]):
        for q in range(sub):
            out_ref[j, :, q * 256:(q + 1) * 256] = acc[j * sub + q].astype(BF)


def graph_partial(place, rows, cols, near, far, blocks, owners, fetched):
    n_slots, side, _ = blocks.shape
    r, width = near.shape[1:]
    sub = width // side
    own = [pltpu.VMEM((n_slots, side, side), BF), pltpu.SemaphoreType.DMA((n_slots // CHUNK,))]
    return pl.pallas_call(
        graph_kernel,
        out_shape=jax.ShapeDtypeStruct((owners, r, width), BF),
        in_specs=[SMEM] * 3 + [VMEM] * 2 + [pl.BlockSpec(memory_space=pltpu.HBM) if fetched else VMEM],
        out_specs=VMEM,
        scratch_shapes=[
            pltpu.VMEM((8 * sub, r, side), BF),
            pltpu.VMEM((owners * sub + 1, r, side), F32),
        ] + (own if fetched else []),
        compiler_params=pltpu.CompilerParams(vmem_limit_bytes=(50 if fetched else 14) * 2**20),
        name="graph_partial",
    )(place, rows, cols, near, far, blocks)


def halves(a):
    top = a.astype(BF)
    return top, (a - top.astype(F32)).astype(BF)


def three(a, b):
    ah, al = halves(a)
    bh, bl = halves(b)

    def dot(u, v):
        return lax.dot_general(u, v, (((1,), (0,)), ((), ())), preferred_element_type=F32)

    return dot(ah, bh) + (dot(ah, bl) + dot(al, bh))


def eye_mask(n):
    return (lax.broadcasted_iota(jnp.int32, (n, n), 0) == lax.broadcasted_iota(jnp.int32, (n, n), 1))


def sweep_inverse(ref):
    n = ref.shape[0]
    ri = lax.broadcasted_iota(jnp.int32, (n, n), 0)
    ci = lax.broadcasted_iota(jnp.int32, (n, n), 1)

    def step(k, carry):
        a = ref[...]
        col = jnp.sum(jnp.where(ci == k, a, 0.0), axis=1, keepdims=True)
        row = jnp.sum(jnp.where(ri == k, a, 0.0), axis=0, keepdims=True)
        pivot = jnp.sum(jnp.where(ci[:1] == k, row, 0.0), axis=1, keepdims=True)
        col = jnp.where(ri[:, :1] == k, -1.0, col)
        row = jnp.where(ci[:1] == k, -1.0, row) / pivot
        ref[...] = jnp.where((ri == k) | (ci == k), 0.0, a) - col * row
        return carry

    lax.fori_loop(0, n, step, 0)
    ref[...] = -ref[...]


def square_sum(a):
    return jnp.sum(a * a)


def spd_inverses(mats, refs):
    scaled, lefts, rights, errs, sums = [], [], [], [], []
    for a in mats:
        eye = eye_mask(a.shape[0])
        diag = jnp.where(eye, a, 0.0)
        left = lax.rsqrt(jnp.sum(diag, axis=1, keepdims=True))
        right = lax.rsqrt(jnp.sum(diag, axis=0, keepdims=True))
        a = a * left * right
        rows = jnp.sum(jnp.abs(a), axis=0, keepdims=True)
        inv = 1.0 / jnp.max(rows, axis=1, keepdims=True)
        unit = eye.astype(F32)
        err = unit - a * inv
        scaled.append(a)
        lefts.append(left)
        rights.append(right)
        errs.append(err)
        sums.append((unit + err) * inv)

    def levels(errs, sums, count):
        for _ in range(count):
            errs = [nn(e, e) for e in errs]
            sums = [s + nn(s, e) for s, e in zip(sums, errs)]
        for (err_ref, sum_ref), e, s in zip(refs, errs, sums):
            err_ref[...] = e
            sum_ref[...] = s
        return sum(square_sum(e) for e in errs)

    def body(state):
        level, _ = state
        size = levels([r[0][...] for r in refs], [r[1][...] for r in refs], 2)
        return level + 1, size

    size = levels(errs, sums, 4)
    _, size = lax.while_loop(lambda s: (s[1] > 1e-8) & (s[0] < 12), body, (jnp.int32(0), size))
    good = size <= 1e-8

    @pl.when(jnp.logical_not(good))
    def _():
        for a, (_, sum_ref) in zip(scaled, refs):
            sum_ref[...] = a
            sweep_inverse(sum_ref)

    return [left * r[1][...] * right for left, right, r in zip(lefts, rights, refs)]


def sign_rows(sym, inverse, cutoff, wanted):
    eye = eye_mask(sym.shape[0]).astype(F32)
    s = (cutoff - 1.0) * eye + nn(sym, inverse)
    s2 = nn(s, s)
    total = jnp.sum(jnp.sum(s2 * eye, axis=1, keepdims=True), axis=0, keepdims=True)
    scale = lax.rsqrt(total + 1e-06)
    s = s * scale
    s2 = s2 * (scale * scale)
    s = 1.5 * s - 0.5 * three(s, s2)
    for _ in range(NS_STEPS - 1):
        s = 1.5 * s - 0.5 * three(s, three(s, s))
    return 0.5 * (eye + s)[:wanted]


def shift(v, wanted):
    return pltpu.roll(v, 2 * wanted, 1)


def fill_gram(packed, full, w):
    full[...] = jnp.zeros_like(full)

    def put(i, j, block):
        full[i * w:(i + 1) * w, j * w:(j + 1) * w] = block
        if i != j:
            full[j * w:(j + 1) * w, i * w:(i + 1) * w] = block.T

    for row, i in enumerate((0, 4, 5, 6)):
        for j in range(4):
            put(i, j, packed[row * w:(row + 1) * w, j * w:(j + 1) * w])
    for row, spots in ((4, ((1, 1), (1, 2), (1, 3), (4, 4))), (5, ((2, 2), (2, 3), (3, 3), (5, 4)))):
        for place, (i, j) in enumerate(spots):
            put(i, j, packed[row * w:(row + 1) * w, place * w:(place + 1) * w])
    q = w // 4
    put(6, 4, jnp.concatenate([packed[6 * w:6 * w + q, n * w:(n + 1) * w] for n in range(4)], 0))


def next_block(rows, basis, gram, inverse_x, w):
    zt = nn(gram[2 * w:, :w], inverse_x)
    x = nn(rows, basis)
    return x, x - nn(rows[:, :w] + nn(rows[:, 2 * w:], zt), basis[:w])


def small_kernel(w, cut_ref, core_ref, mine_ref, other_ref, *rest):
    parts, outs, (full, e96, s96, e32, s32) = rest[:7], rest[7:11], rest[11:]
    refs = [(e96, s96), (e32, s32)]
    mine, other = mine_ref[...], other_ref[...]
    first = core_ref[0] == 0
    fill_gram(jnp.concatenate([jnp.where(first, mine, other), jnp.where(first, other, mine)], 0), full, w)
    width = full.shape[0]
    gram = full[:3 * w, :3 * w]
    sym = 0.5 * (full[:3 * w, 2 * w:5 * w] + full[2 * w:5 * w, :3 * w])
    basis = (lax.broadcasted_iota(jnp.int32, (3 * w, width), 0)
             == lax.broadcasted_iota(jnp.int32, (3 * w, width), 1)).astype(F32)
    for _ in range(ITERS - 1):
        inverse, inverse_x = spd_inverses([gram, gram[:w, :w]], refs)
        rows = sign_rows(sym, inverse, cut_ref[0], w)
        x, p = next_block(rows, basis, gram, inverse_x, w)
        basis = jnp.concatenate([x, p, shift(x, w)], 0)
        tb = nn(basis, full[...])
        moved = shift(basis, w)
        gram = nt(tb, basis)
        sym = 0.5 * (nt(tb, moved) + nt(moved, tb))
    inverse, inverse_x = spd_inverses([gram, gram[:w, :w]], refs)
    rows = sign_rows(sym, inverse, cut_ref[0], w)
    x, p = next_block(rows, basis, gram, inverse_x, w)
    tx = nn(rows, tb)
    moved = shift(x, w)
    (inverse_x,) = spd_inverses([nt(tx, x)], refs[1:])
    zt = nn(nt(moved, tx), inverse_x)
    coeffs = jnp.concatenate([x, p, nn(zt, x) - moved, p - shift(p, w)], 0)
    krylov = jnp.concatenate([r[...] for r in parts] + [jnp.zeros_like(parts[0])], 0)
    found = nn(coeffs, krylov)
    for n, out_ref in enumerate(outs):
        out_ref[...] = found[n * w:(n + 1) * w]


def small(cutoff, core, mine, other, parts):
    w = parts[0].shape[0]
    return pl.pallas_call(
        functools.partial(small_kernel, w),
        out_shape=[jax.ShapeDtypeStruct(parts[0].shape, F32)] * 4,
        in_specs=[SMEM, SMEM] + [VMEM] * 9,
        out_specs=[VMEM] * 4,
        scratch_shapes=[pltpu.VMEM((n, n), F32) for n in (8 * w, 3 * w, 3 * w, w, w)],
        compiler_params=pltpu.CompilerParams(vmem_limit_bytes=16 * 2**20),
        name="small_matrices",
    )(cutoff, core, mine, other, *parts)


def gram_kernel(*refs):
    k = [r[...] for r in refs[:-1]]
    out_ref = refs[-1]
    w = k[0].shape[0]
    out_ref[:4 * w] = nt(jnp.concatenate([k[0], k[4], k[5], k[6]], 0), jnp.concatenate(k[:4], 0))
    inner = jnp.concatenate(k[1:4], 0)
    inner = nt(inner, inner)
    outer = nt(jnp.concatenate(k[4:], 0), k[4])
    out_ref[4 * w:5 * w] = jnp.concatenate([inner[:w], outer[:w]], 1)
    out_ref[5 * w:6 * w] = jnp.concatenate([inner[w:2 * w, w:], inner[2 * w:, 2 * w:], outer[w:2 * w]], 1)
    q = w // 4
    last = outer[2 * w:]
    out_ref[6 * w:6 * w + q] = jnp.concatenate([last[n * q:(n + 1) * q] for n in range(4)], 1)
    out_ref[6 * w + q:] = jnp.zeros_like(out_ref[6 * w + q:])


def packed_gram(blocks):
    w = blocks[0].shape[0]
    return pl.pallas_call(
        gram_kernel,
        out_shape=jax.ShapeDtypeStruct((6 * w + w // 2, 4 * w), F32),
        in_specs=[VMEM] * len(blocks),
        out_specs=VMEM,
        compiler_params=pltpu.CompilerParams(vmem_limit_bytes=16 * 2**20),
        name="packed_gram",
    )(*blocks)


def z_turn(k):
    return [(i, (i + 2 * k) % 8) for i in range(8)]


def y_turn(k):
    return [(i, (i // 4) * 4 + (i + k) % 4) for i in range(16)]


def x_turn(k):
    return [(i, (i + 4 * k) % 16) for i in range(16)]


CORE = [(i, i ^ 1) for i in range(8)]


def gather_brow(v):
    near = jnp.stack([v] + [lax.ppermute(v, "brow", z_turn(k)) for k in (1, 2, 3)])
    return near, lax.ppermute(near, "brow", CORE)


def sum_all(g):
    half = g.shape[0] // 2
    me = lax.axis_index("brow") % 2
    mine = lax.dynamic_slice_in_dim(g, me * half, half, 0)
    other = lax.dynamic_slice_in_dim(g, (1 - me) * half, half, 0)
    v = mine + lax.ppermute(other, "brow", CORE)
    for axis, turn in (("brow", z_turn), ("bcol", y_turn), ("bcol", x_turn)):
        a, b, c = [lax.ppermute(v, axis, turn(k)) for k in (1, 2, 3)]
        v = (v + a) + (b + c)
    return v, lax.ppermute(v, "brow", CORE)


def local(blocks, pattern_rows, pattern_cols, live_count, degree_scale, eigen_block, direction, cutoff):
    block_set = blocks[0, 0]
    wanted = eigen_block.shape[0]
    owners = lax.axis_size("bcol")
    brow = lax.axis_index("brow")
    place = jnp.stack([live_count[0, 0], brow])
    rows, cols = pattern_rows[0, 0], pattern_cols[0, 0]

    def apply_graph(v, fetched=False):
        near, far = gather_brow((degree_scale * v).astype(BF))
        part = graph_partial(place, rows, cols, near, far, block_set, owners, fetched)
        got = lax.all_to_all(part, "bcol", 0, 0)
        return degree_scale * jnp.sum(got.astype(F32), axis=0)

    k1 = apply_graph(jnp.concatenate([eigen_block, direction], 0), True)
    k2 = apply_graph(k1)
    k3 = apply_graph(k2[:wanted])
    parts = [eigen_block, direction, k1[:wanted], k1[wanted:], k2[:wanted], k2[wanted:], k3]
    mine, other = sum_all(packed_gram(parts))
    return tuple(small(cutoff, (brow % 2).reshape(1), mine, other, parts))


def solution(mesh):
    docs = P(None, ("brow", "bcol"))
    return jax.shard_map(
        local,
        mesh=mesh,
        in_specs=(
            P("brow", "bcol", None, None, None),
            P("brow", "bcol", None),
            P("brow", "bcol", None),
            P("brow", "bcol"),
            P(("brow", "bcol")),
            docs,
            docs,
            P(),
        ),
        out_specs=(docs, docs, docs, docs),
        check_vma=False,
    )
```

```python
import functools

import jax
import jax.numpy as jnp
from jax import lax
from jax.experimental import pallas as pl
from jax.experimental.pallas import tpu as pltpu
from jax.sharding import PartitionSpec as P

ITERS = 2
NS_STEPS = 8
CHUNK = 8
HIGH = lax.Precision.HIGHEST
BF = jnp.bfloat16
F32 = jnp.float32
SMEM = pl.BlockSpec(memory_space=pltpu.SMEM)
VMEM = pl.BlockSpec(memory_space=pltpu.VMEM)


def nn(a, b):
    return lax.dot_general(a, b, (((1,), (0,)), ((), ())), precision=HIGH, preferred_element_type=F32)


def nt(a, b):
    return lax.dot_general(a, b, (((1,), (1,)), ((), ())), precision=HIGH, preferred_element_type=F32)


def graph_kernel(table_ref, near_ref, far_ref, blocks_ref, out_ref, panel, acc, *own):
    n_slots = blocks_ref.shape[0]
    live = table_ref[2 * n_slots]
    sub = panel.shape[0] // 8
    chunks = n_slots // CHUNK
    held = own[0] if own else blocks_ref

    def fetch(c):
        part = pl.ds(c * CHUNK, CHUNK)
        return pltpu.make_async_copy(blocks_ref.at[part], held.at[part], own[1].at[c])

    for c in range(chunks if own else 0):
        @pl.when(c * CHUNK < live)
        def _():
            fetch(c).start()

    for s in range(8):
        src = near_ref if s < 4 else far_ref
        for q in range(sub):
            panel[s * sub + q] = src[s % 4, :, q * 256:(q + 1) * 256]
    acc[...] = jnp.zeros_like(acc)

    for c in range(chunks):
        @pl.when(c * CHUNK < live)
        def _():
            if own:
                fetch(c).wait()
            slots = range(c * CHUNK, (c + 1) * CHUNK)
            prods = [lax.dot_general(panel[table_ref[n_slots + s]], held[s], (((1,), (1,)), ((), ())),
                                     preferred_element_type=F32) for s in slots]
            for s, prod in zip(slots, prods):
                row = table_ref[s]
                acc[row] = acc[row] + prod
    for j in range(out_ref.shape[0]):
        for q in range(sub):
            out_ref[j, :, q * 256:(q + 1) * 256] = acc[j * sub + q].astype(BF)


def graph_partial(table, near, far, blocks, owners, fetched):
    n_slots, side, _ = blocks.shape
    r, width = near.shape[1:]
    sub = width // side
    own = [pltpu.VMEM((n_slots, side, side), BF), pltpu.SemaphoreType.DMA((n_slots // CHUNK,))]
    return pl.pallas_call(
        graph_kernel,
        out_shape=jax.ShapeDtypeStruct((owners, r, width), BF),
        in_specs=[SMEM] + [VMEM] * 2 + [pl.BlockSpec(memory_space=pltpu.HBM) if fetched else VMEM],
        out_specs=VMEM,
        scratch_shapes=[
            pltpu.VMEM((8 * sub, r, side), BF),
            pltpu.VMEM((owners * sub + 1, r, side), F32),
        ] + (own if fetched else []),
        compiler_params=pltpu.CompilerParams(vmem_limit_bytes=(50 if fetched else 14) * 2**20),
        name="graph_partial",
    )(table, near, far, blocks)


def halves(a):
    top = a.astype(BF)
    return top, (a - top.astype(F32)).astype(BF)


def three(a, b):
    ah, al = halves(a)
    bh, bl = halves(b)

    def dot(u, v):
        return lax.dot_general(u, v, (((1,), (0,)), ((), ())), preferred_element_type=F32)

    return dot(ah, bh) + (dot(ah, bl) + dot(al, bh))


def eye_mask(n):
    return (lax.broadcasted_iota(jnp.int32, (n, n), 0) == lax.broadcasted_iota(jnp.int32, (n, n), 1))


def sweep_inverse(ref):
    n = ref.shape[0]
    ri = lax.broadcasted_iota(jnp.int32, (n, n), 0)
    ci = lax.broadcasted_iota(jnp.int32, (n, n), 1)

    def step(k, carry):
        a = ref[...]
        col = jnp.sum(jnp.where(ci == k, a, 0.0), axis=1, keepdims=True)
        row = jnp.sum(jnp.where(ri == k, a, 0.0), axis=0, keepdims=True)
        pivot = jnp.sum(jnp.where(ci[:1] == k, row, 0.0), axis=1, keepdims=True)
        col = jnp.where(ri[:, :1] == k, -1.0, col)
        row = jnp.where(ci[:1] == k, -1.0, row) / pivot
        ref[...] = jnp.where((ri == k) | (ci == k), 0.0, a) - col * row
        return carry

    lax.fori_loop(0, n, step, 0)
    ref[...] = -ref[...]


def square_sum(a):
    return jnp.sum(a * a)


def spd_inverses(mats, refs):
    scaled, lefts, rights, errs, sums = [], [], [], [], []
    for a in mats:
        eye = eye_mask(a.shape[0])
        diag = jnp.where(eye, a, 0.0)
        left = lax.rsqrt(jnp.sum(diag, axis=1, keepdims=True))
        right = lax.rsqrt(jnp.sum(diag, axis=0, keepdims=True))
        a = a * left * right
        rows = jnp.sum(jnp.abs(a), axis=0, keepdims=True)
        inv = 1.0 / jnp.max(rows, axis=1, keepdims=True)
        unit = eye.astype(F32)
        err = unit - a * inv
        scaled.append(a)
        lefts.append(left)
        rights.append(right)
        errs.append(err)
        sums.append((unit + err) * inv)

    def levels(errs, sums, count):
        for _ in range(count):
            errs = [nn(e, e) for e in errs]
            sums = [s + nn(s, e) for s, e in zip(sums, errs)]
        for (err_ref, sum_ref), e, s in zip(refs, errs, sums):
            err_ref[...] = e
            sum_ref[...] = s
        return sum(square_sum(e) for e in errs)

    def body(state):
        level, _ = state
        size = levels([r[0][...] for r in refs], [r[1][...] for r in refs], 2)
        return level + 1, size

    size = levels(errs, sums, 4)
    _, size = lax.while_loop(lambda s: (s[1] > 1e-8) & (s[0] < 12), body, (jnp.int32(0), size))
    good = size <= 1e-8

    @pl.when(jnp.logical_not(good))
    def _():
        for a, (_, sum_ref) in zip(scaled, refs):
            sum_ref[...] = a
            sweep_inverse(sum_ref)

    return [left * r[1][...] * right for left, right, r in zip(lefts, rights, refs)]


def sign_rows(sym, inverse, cutoff, wanted):
    eye = eye_mask(sym.shape[0]).astype(F32)
    s = (cutoff - 1.0) * eye + nn(sym, inverse)
    s2 = nn(s, s)
    total = jnp.sum(jnp.sum(s2 * eye, axis=1, keepdims=True), axis=0, keepdims=True)
    scale = lax.rsqrt(total + 1e-06)
    s = s * scale
    s2 = s2 * (scale * scale)
    s = 1.5 * s - 0.5 * three(s, s2)
    for _ in range(NS_STEPS - 1):
        s = 1.5 * s - 0.5 * three(s, three(s, s))
    return 0.5 * (eye + s)[:wanted]


def shift(v, wanted):
    return pltpu.roll(v, 2 * wanted, 1)


def fill_gram(packed, full, w):
    full[...] = jnp.zeros_like(full)

    def put(i, j, block):
        full[i * w:(i + 1) * w, j * w:(j + 1) * w] = block
        if i != j:
            full[j * w:(j + 1) * w, i * w:(i + 1) * w] = block.T

    for row, i in enumerate((0, 4, 5, 6)):
        for j in range(4):
            put(i, j, packed[row * w:(row + 1) * w, j * w:(j + 1) * w])
    for row, spots in ((4, ((1, 1), (1, 2), (1, 3), (4, 4))), (5, ((2, 2), (2, 3), (3, 3), (5, 4)))):
        for place, (i, j) in enumerate(spots):
            put(i, j, packed[row * w:(row + 1) * w, place * w:(place + 1) * w])
    q = w // 4
    put(6, 4, jnp.concatenate([packed[6 * w:6 * w + q, n * w:(n + 1) * w] for n in range(4)], 0))


def next_block(rows, basis, gram, inverse_x, width, w):
    zt = nn(gram[2 * w:, :w], inverse_x)
    both = jnp.concatenate([rows, jnp.concatenate([-nn(rows[:, 2 * w:], zt), rows[:, w:]], 1)], 0)
    if basis is None:
        both = jnp.concatenate([both, jnp.zeros((2 * w, width - 3 * w), F32)], 1)
    else:
        both = nn(both, basis)
    return both[:w], both[w:]


def small_kernel(w, cut_ref, core_ref, mine_ref, other_ref, *rest):
    parts, outs, (full, e96, s96, e32, s32) = rest[:7], rest[7:11], rest[11:]
    refs = [(e96, s96), (e32, s32)]
    mine, other = mine_ref[...], other_ref[...]
    first = core_ref[0] == 0
    fill_gram(jnp.concatenate([jnp.where(first, mine, other), jnp.where(first, other, mine)], 0), full, w)
    width = full.shape[0]
    gram = full[:3 * w, :3 * w]
    sym = 0.5 * (full[:3 * w, 2 * w:5 * w] + full[2 * w:5 * w, :3 * w])
    basis = None
    for _ in range(ITERS - 1):
        inverse, inverse_x = spd_inverses([gram, gram[:w, :w]], refs)
        rows = sign_rows(sym, inverse, cut_ref[0], w)
        x, p = next_block(rows, basis, gram, inverse_x, width, w)
        basis = jnp.concatenate([x, p, shift(x, w)], 0)
        tb = nn(basis, full[...])
        moved = shift(basis, w)
        gram = nt(tb, basis)
        sym = 0.5 * (nt(tb, moved) + nt(moved, tb))
    inverse, inverse_x = spd_inverses([gram, gram[:w, :w]], refs)
    rows = sign_rows(sym, inverse, cut_ref[0], w)
    x, p = next_block(rows, basis, gram, inverse_x, width, w)
    tx = nn(rows, tb)
    moved = shift(x, w)
    (inverse_x,) = spd_inverses([nt(tx, x)], refs[1:])
    zt = nn(nt(moved, tx), inverse_x)
    coeffs = jnp.concatenate([x, p, nn(zt, x) - moved, p - shift(p, w)], 0)
    krylov = jnp.concatenate([r[...] for r in parts] + [jnp.zeros_like(parts[0])], 0)
    found = nn(coeffs, krylov)
    for n, out_ref in enumerate(outs):
        out_ref[...] = found[n * w:(n + 1) * w]


def small(cutoff, core, mine, other, parts):
    w = parts[0].shape[0]
    return pl.pallas_call(
        functools.partial(small_kernel, w),
        out_shape=[jax.ShapeDtypeStruct(parts[0].shape, F32)] * 4,
        in_specs=[SMEM, SMEM] + [VMEM] * 9,
        out_specs=[VMEM] * 4,
        scratch_shapes=[pltpu.VMEM((n, n), F32) for n in (8 * w, 3 * w, 3 * w, w, w)],
        compiler_params=pltpu.CompilerParams(vmem_limit_bytes=16 * 2**20),
        name="small_matrices",
    )(cutoff, core, mine, other, *parts)


def gram_kernel(*refs):
    k = [r[...] for r in refs[:-1]]
    out_ref = refs[-1]
    w = k[0].shape[0]
    out_ref[:4 * w] = nt(jnp.concatenate([k[0], k[4], k[5], k[6]], 0), jnp.concatenate(k[:4], 0))
    inner = jnp.concatenate(k[1:4], 0)
    inner = nt(inner, inner)
    outer = nt(jnp.concatenate(k[4:], 0), k[4])
    out_ref[4 * w:5 * w] = jnp.concatenate([inner[:w], outer[:w]], 1)
    out_ref[5 * w:6 * w] = jnp.concatenate([inner[w:2 * w, w:], inner[2 * w:, 2 * w:], outer[w:2 * w]], 1)
    q = w // 4
    last = outer[2 * w:]
    out_ref[6 * w:6 * w + q] = jnp.concatenate([last[n * q:(n + 1) * q] for n in range(4)], 1)
    out_ref[6 * w + q:] = jnp.zeros_like(out_ref[6 * w + q:])


def packed_gram(blocks):
    w = blocks[0].shape[0]
    return pl.pallas_call(
        gram_kernel,
        out_shape=jax.ShapeDtypeStruct((6 * w + w // 2, 4 * w), F32),
        in_specs=[VMEM] * len(blocks),
        out_specs=VMEM,
        compiler_params=pltpu.CompilerParams(vmem_limit_bytes=16 * 2**20),
        name="packed_gram",
    )(*blocks)


def z_turn(k):
    return [(i, (i + 2 * k) % 8) for i in range(8)]


def y_turn(k):
    return [(i, (i // 4) * 4 + (i + k) % 4) for i in range(16)]


def x_turn(k):
    return [(i, (i + 4 * k) % 16) for i in range(16)]


CORE = [(i, i ^ 1) for i in range(8)]


def gather_brow(v):
    got = {k: lax.ppermute(v, "brow", z_turn(k)) for k in (3, 2, 1)}
    near = jnp.stack([v, got[3], got[1], got[2]])
    return near, lax.ppermute(near, "brow", CORE)


def sum_all(g):
    half = g.shape[0] // 2
    me = lax.axis_index("brow") % 2
    mine = lax.dynamic_slice_in_dim(g, me * half, half, 0)
    other = lax.dynamic_slice_in_dim(g, (1 - me) * half, half, 0)
    v = mine + lax.ppermute(other, "brow", CORE)
    for axis, turn in (("brow", z_turn), ("bcol", y_turn), ("bcol", x_turn)):
        a, b, c = [lax.ppermute(v, axis, turn(k)) for k in (3, 2, 1)]
        v = (v + a) + (b + c)
    return v, lax.ppermute(v, "brow", CORE)


def local(blocks, pattern_rows, pattern_cols, live_count, degree_scale, eigen_block, direction, cutoff):
    block_set = blocks[0, 0]
    wanted = eigen_block.shape[0]
    owners = lax.axis_size("bcol")
    brow = lax.axis_index("brow")
    sub = eigen_block.shape[1] // block_set.shape[-1]
    rows, source, live = pattern_rows[0, 0], pattern_cols[0, 0] // sub, live_count[0, 0]
    rows = jnp.where(jnp.arange(rows.shape[0]) < live, rows, owners * sub)
    turn = (brow // 2 - source // 2) % 4
    place = jnp.where(turn > 0, turn % 3 + 1, 0)
    spots = (place + 4 * ((brow - source) % 2)) * sub + pattern_cols[0, 0] % sub
    table = jnp.concatenate([rows, spots, live.reshape(1)])

    def apply_graph(v, fetched=False):
        near, far = gather_brow((degree_scale * v).astype(BF))
        part = graph_partial(table, near, far, block_set, owners, fetched)
        got = lax.all_to_all(part, "bcol", 0, 0)
        return degree_scale * jnp.sum(got.astype(F32), axis=0)

    k1 = apply_graph(jnp.concatenate([eigen_block, direction], 0), True)
    k2 = apply_graph(k1)
    k3 = apply_graph(k2[:wanted])
    parts = [eigen_block, direction, k1[:wanted], k1[wanted:], k2[:wanted], k2[wanted:], k3]
    mine, other = sum_all(packed_gram(parts))
    return tuple(small(cutoff, (brow % 2).reshape(1), mine, other, parts))


def solution(mesh):
    docs = P(None, ("brow", "bcol"))
    return jax.shard_map(
        local,
        mesh=mesh,
        in_specs=(
            P("brow", "bcol", None, None, None),
            P("brow", "bcol", None),
            P("brow", "bcol", None),
            P("brow", "bcol"),
            P(("brow", "bcol")),
            docs,
            docs,
            P(),
        ),
        out_specs=(docs, docs, docs, docs),
        check_vma=False,
    )
```

```python
import functools

import jax
import jax.numpy as jnp
from jax import lax
from jax.experimental import pallas as pl
from jax.experimental.pallas import tpu as pltpu
from jax.sharding import PartitionSpec as P

ITERS = 2
NS_STEPS = 8
CHUNK = 8
HIGH = lax.Precision.HIGHEST
BF = jnp.bfloat16
F32 = jnp.float32
SMEM = pl.BlockSpec(memory_space=pltpu.SMEM)
VMEM = pl.BlockSpec(memory_space=pltpu.VMEM)


def nn(a, b):
    return lax.dot_general(a, b, (((1,), (0,)), ((), ())), precision=HIGH, preferred_element_type=F32)


def nt(a, b):
    return lax.dot_general(a, b, (((1,), (1,)), ((), ())), precision=HIGH, preferred_element_type=F32)


def graph_kernel(table_ref, near_ref, far_ref, blocks_ref, out_ref, panel, acc, *own):
    n_slots = blocks_ref.shape[0]
    live = table_ref[2 * n_slots]
    sub = panel.shape[0] // 8
    chunks = n_slots // CHUNK
    held = own[0] if own else blocks_ref

    def fetch(c):
        part = pl.ds(c * CHUNK, CHUNK)
        return pltpu.make_async_copy(blocks_ref.at[part], held.at[part], own[1].at[c])

    for c in range(chunks if own else 0):
        @pl.when(c * CHUNK < live)
        def _():
            fetch(c).start()

    for s in range(8):
        src = near_ref if s < 4 else far_ref
        for q in range(sub):
            panel[s * sub + q] = src[s % 4, :, q * 256:(q + 1) * 256]
    acc[...] = jnp.zeros_like(acc)

    for c in range(chunks):
        @pl.when(c * CHUNK < live)
        def _():
            if own:
                fetch(c).wait()
            slots = range(c * CHUNK, (c + 1) * CHUNK)
            prods = [lax.dot_general(panel[table_ref[n_slots + s]], held[s], (((1,), (1,)), ((), ())),
                                     preferred_element_type=F32) for s in slots]
            for s, prod in zip(slots, prods):
                row = table_ref[s]
                acc[row] = acc[row] + prod
    for j in range(out_ref.shape[0]):
        for q in range(sub):
            out_ref[j, :, q * 256:(q + 1) * 256] = acc[j * sub + q].astype(BF)


def graph_partial(table, near, far, blocks, owners, fetched):
    n_slots, side, _ = blocks.shape
    r, width = near.shape[1:]
    sub = width // side
    own = [pltpu.VMEM((n_slots, side, side), BF), pltpu.SemaphoreType.DMA((n_slots // CHUNK,))]
    return pl.pallas_call(
        graph_kernel,
        out_shape=jax.ShapeDtypeStruct((owners, r, width), BF),
        in_specs=[SMEM] + [VMEM] * 2 + [pl.BlockSpec(memory_space=pltpu.HBM) if fetched else VMEM],
        out_specs=VMEM,
        scratch_shapes=[
            pltpu.VMEM((8 * sub, r, side), BF),
            pltpu.VMEM((owners * sub + 1, r, side), F32),
        ] + (own if fetched else []),
        compiler_params=pltpu.CompilerParams(vmem_limit_bytes=(50 if fetched else 14) * 2**20),
        name="graph_partial",
    )(table, near, far, blocks)


def halves(a):
    top = a.astype(BF)
    return top, (a - top.astype(F32)).astype(BF)


def three(a, b):
    ah, al = halves(a)
    bh, bl = halves(b)

    def dot(u, v):
        return lax.dot_general(u, v, (((1,), (0,)), ((), ())), preferred_element_type=F32)

    return dot(ah, bh) + (dot(ah, bl) + dot(al, bh))


def eye_mask(n):
    return (lax.broadcasted_iota(jnp.int32, (n, n), 0) == lax.broadcasted_iota(jnp.int32, (n, n), 1))


def sweep_inverse(ref):
    n = ref.shape[0]
    ri = lax.broadcasted_iota(jnp.int32, (n, n), 0)
    ci = lax.broadcasted_iota(jnp.int32, (n, n), 1)

    def step(k, carry):
        a = ref[...]
        col = jnp.sum(jnp.where(ci == k, a, 0.0), axis=1, keepdims=True)
        row = jnp.sum(jnp.where(ri == k, a, 0.0), axis=0, keepdims=True)
        pivot = jnp.sum(jnp.where(ci[:1] == k, row, 0.0), axis=1, keepdims=True)
        col = jnp.where(ri[:, :1] == k, -1.0, col)
        row = jnp.where(ci[:1] == k, -1.0, row) / pivot
        ref[...] = jnp.where((ri == k) | (ci == k), 0.0, a) - col * row
        return carry

    lax.fori_loop(0, n, step, 0)
    ref[...] = -ref[...]


def square_sum(a):
    return jnp.sum(a * a)


def spd_inverses(mats, refs):
    scaled, lefts, rights, errs, sums = [], [], [], [], []
    for a in mats:
        eye = eye_mask(a.shape[0])
        diag = jnp.where(eye, a, 0.0)
        left = lax.rsqrt(jnp.sum(diag, axis=1, keepdims=True))
        right = lax.rsqrt(jnp.sum(diag, axis=0, keepdims=True))
        a = a * left * right
        rows = jnp.sum(jnp.abs(a), axis=0, keepdims=True)
        inv = 1.0 / jnp.max(rows, axis=1, keepdims=True)
        unit = eye.astype(F32)
        err = unit - a * inv
        scaled.append(a)
        lefts.append(left)
        rights.append(right)
        errs.append(err)
        sums.append((unit + err) * inv)

    def levels(errs, sums, count):
        for _ in range(count):
            errs = [nn(e, e) for e in errs]
            sums = [s + nn(s, e) for s, e in zip(sums, errs)]
        for (err_ref, sum_ref), e, s in zip(refs, errs, sums):
            err_ref[...] = e
            sum_ref[...] = s
        return sum(square_sum(e) for e in errs)

    def body(state):
        level, _ = state
        size = levels([r[0][...] for r in refs], [r[1][...] for r in refs], 1)
        return level + 1, size

    size = levels(errs, sums, 4)
    _, size = lax.while_loop(lambda s: (s[1] > 1e-8) & (s[0] < 24), body, (jnp.int32(0), size))
    good = size <= 1e-8

    @pl.when(jnp.logical_not(good))
    def _():
        for a, (_, sum_ref) in zip(scaled, refs):
            sum_ref[...] = a
            sweep_inverse(sum_ref)

    return [left * r[1][...] * right for left, right, r in zip(lefts, rights, refs)]


def sign_rows(sym, inverse, cutoff, wanted):
    eye = eye_mask(sym.shape[0]).astype(F32)
    s = (cutoff - 1.0) * eye + nn(sym, inverse)
    s2 = nn(s, s)
    total = jnp.sum(jnp.sum(s2 * eye, axis=1, keepdims=True), axis=0, keepdims=True)
    scale = lax.rsqrt(total + 1e-06)
    s = s * scale
    s2 = s2 * (scale * scale)
    s = 1.5 * s - 0.5 * three(s, s2)
    for _ in range(NS_STEPS - 1):
        s = 1.5 * s - 0.5 * three(s, three(s, s))
    return 0.5 * (eye + s)[:wanted]


def shift(v, wanted):
    return pltpu.roll(v, 2 * wanted, 1)


def fill_gram(packed, full, w):
    full[...] = jnp.zeros_like(full)

    def put(i, j, block):
        full[i * w:(i + 1) * w, j * w:(j + 1) * w] = block
        if i != j:
            full[j * w:(j + 1) * w, i * w:(i + 1) * w] = block.T

    for row, i in enumerate((0, 4, 5, 6)):
        for j in range(4):
            put(i, j, packed[row * w:(row + 1) * w, j * w:(j + 1) * w])
    for row, spots in ((4, ((1, 1), (1, 2), (1, 3), (4, 4))), (5, ((2, 2), (2, 3), (3, 3), (5, 4)))):
        for place, (i, j) in enumerate(spots):
            put(i, j, packed[row * w:(row + 1) * w, place * w:(place + 1) * w])
    q = w // 4
    put(6, 4, jnp.concatenate([packed[6 * w:6 * w + q, n * w:(n + 1) * w] for n in range(4)], 0))


def next_block(rows, basis, gram, inverse_x, width, w):
    zt = nn(gram[2 * w:, :w], inverse_x)
    both = jnp.concatenate([rows, jnp.concatenate([-nn(rows[:, 2 * w:], zt), rows[:, w:]], 1)], 0)
    if basis is None:
        both = jnp.concatenate([both, jnp.zeros((2 * w, width - 3 * w), F32)], 1)
    else:
        both = nn(both, basis)
    return both[:w], both[w:]


def small_kernel(w, cut_ref, core_ref, mine_ref, other_ref, *rest):
    parts, outs, (full, e96, s96, e32, s32) = rest[:7], rest[7:11], rest[11:]
    refs = [(e96, s96), (e32, s32)]
    mine, other = mine_ref[...], other_ref[...]
    first = core_ref[0] == 0
    fill_gram(jnp.concatenate([jnp.where(first, mine, other), jnp.where(first, other, mine)], 0), full, w)
    width = full.shape[0]
    gram = full[:3 * w, :3 * w]
    sym = 0.5 * (full[:3 * w, 2 * w:5 * w] + full[2 * w:5 * w, :3 * w])
    basis = None
    for _ in range(ITERS - 1):
        inverse, inverse_x = spd_inverses([gram, gram[:w, :w]], refs)
        rows = sign_rows(sym, inverse, cut_ref[0], w)
        x, p = next_block(rows, basis, gram, inverse_x, width, w)
        basis = jnp.concatenate([x, p, shift(x, w)], 0)
        tb = nn(basis, full[...])
        moved = shift(basis, w)
        gram = nt(tb, basis)
        sym = 0.5 * (nt(tb, moved) + nt(moved, tb))
    inverse, inverse_x = spd_inverses([gram, gram[:w, :w]], refs)
    rows = sign_rows(sym, inverse, cut_ref[0], w)
    x, p = next_block(rows, basis, gram, inverse_x, width, w)
    tx = nn(rows, tb)
    moved = shift(x, w)
    (inverse_x,) = spd_inverses([nt(tx, x)], refs[1:])
    zt = nn(nt(moved, tx), inverse_x)
    coeffs = jnp.concatenate([x, p, nn(zt, x) - moved, p - shift(p, w)], 0)
    krylov = jnp.concatenate([r[...] for r in parts] + [jnp.zeros_like(parts[0])], 0)
    found = nn(coeffs, krylov)
    for n, out_ref in enumerate(outs):
        out_ref[...] = found[n * w:(n + 1) * w]


def small(cutoff, core, mine, other, parts):
    w = parts[0].shape[0]
    return pl.pallas_call(
        functools.partial(small_kernel, w),
        out_shape=[jax.ShapeDtypeStruct(parts[0].shape, F32)] * 4,
        in_specs=[SMEM, SMEM] + [VMEM] * 9,
        out_specs=[VMEM] * 4,
        scratch_shapes=[pltpu.VMEM((n, n), F32) for n in (8 * w, 3 * w, 3 * w, w, w)],
        compiler_params=pltpu.CompilerParams(vmem_limit_bytes=16 * 2**20),
        name="small_matrices",
    )(cutoff, core, mine, other, *parts)


def gram_kernel(*refs):
    k = [r[...] for r in refs[:-1]]
    out_ref = refs[-1]
    w = k[0].shape[0]
    out_ref[:3 * w] = nt(jnp.concatenate([k[0], k[4], k[5]], 0), jnp.concatenate(k[:4], 0))
    inner = jnp.concatenate(k[1:4], 0)
    inner = nt(inner, inner)
    outer = nt(jnp.concatenate(k[4:], 0), k[4])
    out_ref[3 * w:4 * w] = jnp.concatenate([inner[:w], outer[:w]], 1)
    out_ref[4 * w:] = jnp.concatenate([inner[w:2 * w, w:], inner[2 * w:, 2 * w:], outer[w:]], 1)


def last_gram_kernel(*refs):
    k = [r[...] for r in refs[:6]]
    found_ref, out_ref = refs[6:]
    w = k[0].shape[0]
    last = nt(k[5], jnp.concatenate(k[:5], 0))
    out_ref[:3 * w] = found_ref[:3 * w]
    out_ref[3 * w:4 * w] = last[:, :4 * w]
    out_ref[4 * w:6 * w] = found_ref[3 * w:]
    q = w // 4
    out_ref[6 * w:6 * w + q] = jnp.concatenate([last[n * q:(n + 1) * q, 4 * w:] for n in range(4)], 1)
    out_ref[6 * w + q:] = jnp.zeros_like(out_ref[6 * w + q:])


def gram_call(kernel, name, rows, *arrays):
    return pl.pallas_call(
        kernel,
        out_shape=jax.ShapeDtypeStruct((rows, 4 * arrays[0].shape[0]), F32),
        in_specs=[VMEM] * len(arrays),
        out_specs=VMEM,
        compiler_params=pltpu.CompilerParams(vmem_limit_bytes=16 * 2**20),
        name=name,
    )(*arrays)


def packed_gram(blocks):
    w = blocks[0].shape[0]
    found = gram_call(gram_kernel, "first_gram", 5 * w, *blocks[:6])
    return gram_call(last_gram_kernel, "packed_gram", 6 * w + w // 2, *blocks[:5], blocks[6], found)


def z_turn(k):
    return [(i, (i + 2 * k) % 8) for i in range(8)]


def y_turn(k):
    return [(i, (i // 4) * 4 + (i + k) % 4) for i in range(16)]


def x_turn(k):
    return [(i, (i + 4 * k) % 16) for i in range(16)]


CORE = [(i, i ^ 1) for i in range(8)]


def gather_brow(v):
    got = {k: lax.ppermute(v, "brow", z_turn(k)) for k in (3, 2, 1)}
    near = jnp.stack([v, got[3], got[1], got[2]])
    return near, lax.ppermute(near, "brow", CORE)


def sum_all(g):
    half = g.shape[0] // 2
    me = lax.axis_index("brow") % 2
    mine = lax.dynamic_slice_in_dim(g, me * half, half, 0)
    other = lax.dynamic_slice_in_dim(g, (1 - me) * half, half, 0)
    v = mine + lax.ppermute(other, "brow", CORE)
    for axis, turn in (("bcol", x_turn), ("brow", z_turn), ("bcol", y_turn)):
        a, b, c = [lax.ppermute(v, axis, turn(k)) for k in (3, 2, 1)]
        v = (v + a) + (b + c)
    return v, lax.ppermute(v, "brow", CORE)


def local(blocks, pattern_rows, pattern_cols, live_count, degree_scale, eigen_block, direction, cutoff):
    block_set = blocks[0, 0]
    wanted = eigen_block.shape[0]
    owners = lax.axis_size("bcol")
    brow = lax.axis_index("brow")
    sub = eigen_block.shape[1] // block_set.shape[-1]
    rows, source, live = pattern_rows[0, 0], pattern_cols[0, 0] // sub, live_count[0, 0]
    rows = jnp.where(jnp.arange(rows.shape[0]) < live, rows, owners * sub)
    turn = (brow // 2 - source // 2) % 4
    place = jnp.where(turn > 0, turn % 3 + 1, 0)
    spots = (place + 4 * ((brow - source) % 2)) * sub + pattern_cols[0, 0] % sub
    table = jnp.concatenate([rows, spots, live.reshape(1)])

    def apply_graph(v, fetched=False):
        near, far = gather_brow((degree_scale * v).astype(BF))
        part = graph_partial(table, near, far, block_set, owners, fetched)
        got = lax.all_to_all(part, "bcol", 0, 0)
        return degree_scale * jnp.sum(got.astype(F32), axis=0)

    k1 = apply_graph(jnp.concatenate([eigen_block, direction], 0), True)
    k2 = apply_graph(k1)
    k3 = apply_graph(k2[:wanted])
    parts = [eigen_block, direction, k1[:wanted], k1[wanted:], k2[:wanted], k2[wanted:], k3]
    mine, other = sum_all(packed_gram(parts))
    return tuple(small(cutoff, (brow % 2).reshape(1), mine, other, parts))


def solution(mesh):
    docs = P(None, ("brow", "bcol"))
    return jax.shard_map(
        local,
        mesh=mesh,
        in_specs=(
            P("brow", "bcol", None, None, None),
            P("brow", "bcol", None),
            P("brow", "bcol", None),
            P("brow", "bcol"),
            P(("brow", "bcol")),
            docs,
            docs,
            P(),
        ),
        out_specs=(docs, docs, docs, docs),
        check_vma=False,
    )
```

```python
import functools

import jax
import jax.numpy as jnp
from jax import lax
from jax.experimental import pallas as pl
from jax.experimental.pallas import tpu as pltpu
from jax.sharding import PartitionSpec as P

ITERS = 2
NS_STEPS = 8
CHUNK = 8
HIGH = lax.Precision.HIGHEST
BF = jnp.bfloat16
F32 = jnp.float32
SMEM = pl.BlockSpec(memory_space=pltpu.SMEM)
VMEM = pl.BlockSpec(memory_space=pltpu.VMEM)


def nn(a, b):
    return lax.dot_general(a, b, (((1,), (0,)), ((), ())), precision=HIGH, preferred_element_type=F32)


def nt(a, b):
    return lax.dot_general(a, b, (((1,), (1,)), ((), ())), precision=HIGH, preferred_element_type=F32)


def graph_kernel(n_out, table_ref, near_ref, far_ref, blocks_ref, *rest):
    outs, (panel, acc, *own) = rest[:n_out], rest[n_out:]
    n_slots = blocks_ref.shape[0]
    live = table_ref[2 * n_slots]
    sub = panel.shape[0] // 8
    chunks = n_slots // CHUNK
    held = own[0] if own else blocks_ref

    def fetch(c):
        part = pl.ds(c * CHUNK, CHUNK)
        return pltpu.make_async_copy(blocks_ref.at[part], held.at[part], own[1].at[c])

    for c in range(chunks if own else 0):
        @pl.when(c * CHUNK < live)
        def _():
            fetch(c).start()

    for s in range(8):
        src = near_ref if s < 4 else far_ref
        for q in range(sub):
            panel[s * sub + q] = src[s % 4, :, q * 256:(q + 1) * 256]
    acc[...] = jnp.zeros_like(acc)

    for c in range(chunks):
        @pl.when(c * CHUNK < live)
        def _():
            if own:
                fetch(c).wait()
            slots = range(c * CHUNK, (c + 1) * CHUNK)
            prods = [lax.dot_general(panel[table_ref[n_slots + s]], held[s], (((1,), (1,)), ((), ())),
                                     preferred_element_type=F32) for s in slots]
            for s, prod in zip(slots, prods):
                row = table_ref[s]
                acc[row] = acc[row] + prod
    if n_out == 1:
        out_ref = outs[0]
        for j in range(out_ref.shape[0]):
            for q in range(sub):
                out_ref[j, :, q * 256:(q + 1) * 256] = acc[j * sub + q].astype(BF)
        return
    mx, my = table_ref[2 * n_slots + 1], table_ref[2 * n_slots + 2]
    half = acc.shape[1] // 2
    for k in range(4):
        for m in range(4):
            for_x = jnp.bitwise_and(mx + k, 3) * 4 + jnp.bitwise_and(my + m, 3)
            for_p = jnp.bitwise_and(mx + m, 3) * 4 + jnp.bitwise_and(my + k, 3)
            for q in range(sub):
                columns = pl.ds(q * 256, 256)
                outs[k][m, :, columns] = acc[for_x * sub + q, :half].astype(BF)
                outs[4 + k][m, :, columns] = acc[for_p * sub + q, half:].astype(BF)


def graph_partial(table, near, far, blocks, owners, fetched, split=False):
    n_slots, side, _ = blocks.shape
    r, width = near.shape[1:]
    sub = width // side
    own = [pltpu.VMEM((n_slots, side, side), BF), pltpu.SemaphoreType.DMA((n_slots // CHUNK,))]
    return pl.pallas_call(
        functools.partial(graph_kernel, 8 if split else 1),
        out_shape=([jax.ShapeDtypeStruct((4, r // 2, width), BF)] * 8 if split
                   else jax.ShapeDtypeStruct((owners, r, width), BF)),
        in_specs=[SMEM] + [VMEM] * 2 + [pl.BlockSpec(memory_space=pltpu.HBM) if fetched else VMEM],
        out_specs=[VMEM] * 8 if split else VMEM,
        scratch_shapes=[
            pltpu.VMEM((8 * sub, r, side), BF),
            pltpu.VMEM((owners * sub + 1, r, side), F32),
        ] + (own if fetched else []),
        compiler_params=pltpu.CompilerParams(vmem_limit_bytes=(50 if fetched else 14) * 2**20),
        name="graph_partial",
    )(table, near, far, blocks)


def halves(a):
    top = a.astype(BF)
    return top, (a - top.astype(F32)).astype(BF)


def three(a, b):
    ah, al = halves(a)
    bh, bl = halves(b)

    def dot(u, v):
        return lax.dot_general(u, v, (((1,), (0,)), ((), ())), preferred_element_type=F32)

    return dot(ah, bh) + (dot(ah, bl) + dot(al, bh))


def eye_mask(n):
    return (lax.broadcasted_iota(jnp.int32, (n, n), 0) == lax.broadcasted_iota(jnp.int32, (n, n), 1))


def sweep_inverse(ref):
    n = ref.shape[0]
    ri = lax.broadcasted_iota(jnp.int32, (n, n), 0)
    ci = lax.broadcasted_iota(jnp.int32, (n, n), 1)

    def step(k, carry):
        a = ref[...]
        col = jnp.sum(jnp.where(ci == k, a, 0.0), axis=1, keepdims=True)
        row = jnp.sum(jnp.where(ri == k, a, 0.0), axis=0, keepdims=True)
        pivot = jnp.sum(jnp.where(ci[:1] == k, row, 0.0), axis=1, keepdims=True)
        col = jnp.where(ri[:, :1] == k, -1.0, col)
        row = jnp.where(ci[:1] == k, -1.0, row) / pivot
        ref[...] = jnp.where((ri == k) | (ci == k), 0.0, a) - col * row
        return carry

    lax.fori_loop(0, n, step, 0)
    ref[...] = -ref[...]


def square_sum(a):
    return jnp.sum(a * a)


def spd_inverses(mats, refs):
    scaled, lefts, rights, errs, sums = [], [], [], [], []
    for a in mats:
        eye = eye_mask(a.shape[0])
        diag = jnp.where(eye, a, 0.0)
        left = lax.rsqrt(jnp.sum(diag, axis=1, keepdims=True))
        right = lax.rsqrt(jnp.sum(diag, axis=0, keepdims=True))
        a = a * left * right
        rows = jnp.sum(jnp.abs(a), axis=0, keepdims=True)
        inv = 1.0 / jnp.max(rows, axis=1, keepdims=True)
        unit = eye.astype(F32)
        err = unit - a * inv
        scaled.append(a)
        lefts.append(left)
        rights.append(right)
        errs.append(err)
        sums.append((unit + err) * inv)

    def levels(errs, sums, count):
        for _ in range(count):
            errs = [nn(e, e) for e in errs]
            sums = [s + nn(s, e) for s, e in zip(sums, errs)]
        for (err_ref, sum_ref), e, s in zip(refs, errs, sums):
            err_ref[...] = e
            sum_ref[...] = s
        return sum(square_sum(e) for e in errs)

    def body(state):
        level, _ = state
        size = levels([r[0][...] for r in refs], [r[1][...] for r in refs], 1)
        return level + 1, size

    size = levels(errs, sums, 4)
    _, size = lax.while_loop(lambda s: (s[1] > 1e-8) & (s[0] < 24), body, (jnp.int32(0), size))
    good = size <= 1e-8

    @pl.when(jnp.logical_not(good))
    def _():
        for a, (_, sum_ref) in zip(scaled, refs):
            sum_ref[...] = a
            sweep_inverse(sum_ref)

    return [left * r[1][...] * right for left, right, r in zip(lefts, rights, refs)]


def sign_rows(sym, inverse, cutoff, wanted):
    eye = eye_mask(sym.shape[0]).astype(F32)
    s = (cutoff - 1.0) * eye + nn(sym, inverse)
    s2 = nn(s, s)
    total = jnp.sum(jnp.sum(s2 * eye, axis=1, keepdims=True), axis=0, keepdims=True)
    scale = lax.rsqrt(total + 1e-06)
    s = s * scale
    s2 = s2 * (scale * scale)
    s = 1.5 * s - 0.5 * three(s, s2)
    for _ in range(NS_STEPS - 1):
        s = 1.5 * s - 0.5 * three(s, three(s, s))
    return 0.5 * (eye + s)[:wanted]


def shift(v, wanted):
    return pltpu.roll(v, 2 * wanted, 1)


def fill_gram(packed, full, w):
    full[...] = jnp.zeros_like(full)

    def put(i, j, block):
        full[i * w:(i + 1) * w, j * w:(j + 1) * w] = block
        if i != j:
            full[j * w:(j + 1) * w, i * w:(i + 1) * w] = block.T

    for row, i in enumerate((0, 4, 5, 6)):
        for j in range(4):
            put(i, j, packed[row * w:(row + 1) * w, j * w:(j + 1) * w])
    for row, spots in ((4, ((1, 1), (1, 2), (1, 3), (4, 4))), (5, ((2, 2), (2, 3), (3, 3), (5, 4)))):
        for place, (i, j) in enumerate(spots):
            put(i, j, packed[row * w:(row + 1) * w, place * w:(place + 1) * w])
    q = w // 4
    put(6, 4, jnp.concatenate([packed[6 * w:6 * w + q, n * w:(n + 1) * w] for n in range(4)], 0))


def next_block(rows, basis, gram, inverse_x, width, w):
    zt = nn(gram[2 * w:, :w], inverse_x)
    both = jnp.concatenate([rows, jnp.concatenate([-nn(rows[:, 2 * w:], zt), rows[:, w:]], 1)], 0)
    if basis is None:
        both = jnp.concatenate([both, jnp.zeros((2 * w, width - 3 * w), F32)], 1)
    else:
        both = nn(both, basis)
    return both[:w], both[w:]


def small_kernel(w, cut_ref, core_ref, mine_ref, other_ref, *rest):
    parts, outs, (full, e96, s96, e32, s32) = rest[:7], rest[7:11], rest[11:]
    refs = [(e96, s96), (e32, s32)]
    mine, other = mine_ref[...], other_ref[...]
    first = core_ref[0] == 0
    fill_gram(jnp.concatenate([jnp.where(first, mine, other), jnp.where(first, other, mine)], 0), full, w)
    width = full.shape[0]
    gram = full[:3 * w, :3 * w]
    sym = 0.5 * (full[:3 * w, 2 * w:5 * w] + full[2 * w:5 * w, :3 * w])
    basis = None
    for _ in range(ITERS - 1):
        inverse, inverse_x = spd_inverses([gram, gram[:w, :w]], refs)
        rows = sign_rows(sym, inverse, cut_ref[0], w)
        x, p = next_block(rows, basis, gram, inverse_x, width, w)
        basis = jnp.concatenate([x, p, shift(x, w)], 0)
        tb = nn(basis, full[...])
        moved = shift(basis, w)
        gram = nt(tb, basis)
        sym = 0.5 * (nt(tb, moved) + nt(moved, tb))
    inverse, inverse_x = spd_inverses([gram, gram[:w, :w]], refs)
    rows = sign_rows(sym, inverse, cut_ref[0], w)
    x, p = next_block(rows, basis, gram, inverse_x, width, w)
    tx = nn(rows, tb)
    moved = shift(x, w)
    (inverse_x,) = spd_inverses([nt(tx, x)], refs[1:])
    zt = nn(nt(moved, tx), inverse_x)
    coeffs = jnp.concatenate([x, p, nn(zt, x) - moved, p - shift(p, w)], 0)
    krylov = jnp.concatenate([r[...] for r in parts] + [jnp.zeros_like(parts[0])], 0)
    found = nn(coeffs, krylov)
    for n, out_ref in enumerate(outs):
        out_ref[...] = found[n * w:(n + 1) * w]


def small(cutoff, core, mine, other, parts):
    w = parts[0].shape[0]
    return pl.pallas_call(
        functools.partial(small_kernel, w),
        out_shape=[jax.ShapeDtypeStruct(parts[0].shape, F32)] * 4,
        in_specs=[SMEM, SMEM] + [VMEM] * 9,
        out_specs=[VMEM] * 4,
        scratch_shapes=[pltpu.VMEM((n, n), F32) for n in (8 * w, 3 * w, 3 * w, w, w)],
        compiler_params=pltpu.CompilerParams(vmem_limit_bytes=16 * 2**20),
        name="small_matrices",
    )(cutoff, core, mine, other, *parts)


def gram_kernel(*refs):
    k = [r[...] for r in refs[:-1]]
    out_ref = refs[-1]
    w = k[0].shape[0]
    out_ref[:3 * w] = nt(jnp.concatenate([k[0], k[4], k[5]], 0), jnp.concatenate(k[:4], 0))
    inner = jnp.concatenate(k[1:4], 0)
    inner = nt(inner, inner)
    outer = nt(jnp.concatenate(k[4:], 0), k[4])
    out_ref[3 * w:4 * w] = jnp.concatenate([inner[:w], outer[:w]], 1)
    out_ref[4 * w:] = jnp.concatenate([inner[w:2 * w, w:], inner[2 * w:, 2 * w:], outer[w:]], 1)


def last_gram_kernel(*refs):
    k = [r[...] for r in refs[:6]]
    found_ref, out_ref = refs[6:]
    w = k[0].shape[0]
    last = nt(k[5], jnp.concatenate(k[:5], 0))
    out_ref[:3 * w] = found_ref[:3 * w]
    out_ref[3 * w:4 * w] = last[:, :4 * w]
    out_ref[4 * w:6 * w] = found_ref[3 * w:]
    q = w // 4
    out_ref[6 * w:6 * w + q] = jnp.concatenate([last[n * q:(n + 1) * q, 4 * w:] for n in range(4)], 1)
    out_ref[6 * w + q:] = jnp.zeros_like(out_ref[6 * w + q:])


def gram_call(kernel, name, rows, *arrays):
    return pl.pallas_call(
        kernel,
        out_shape=jax.ShapeDtypeStruct((rows, 4 * arrays[0].shape[0]), F32),
        in_specs=[VMEM] * len(arrays),
        out_specs=VMEM,
        compiler_params=pltpu.CompilerParams(vmem_limit_bytes=16 * 2**20),
        name=name,
    )(*arrays)


def packed_gram(blocks):
    w = blocks[0].shape[0]
    found = gram_call(gram_kernel, "first_gram", 5 * w, *blocks[:6])
    return gram_call(last_gram_kernel, "packed_gram", 6 * w + w // 2, *blocks[:5], blocks[6], found)


def z_turn(k):
    return [(i, (i + 2 * k) % 8) for i in range(8)]


def y_turn(k):
    return [(i, (i // 4) * 4 + (i + k) % 4) for i in range(16)]


def x_turn(k):
    return [(i, (i + 4 * k) % 16) for i in range(16)]


CORE = [(i, i ^ 1) for i in range(8)]


def gather_brow(v):
    got = {k: lax.ppermute(v, "brow", z_turn(k)) for k in (3, 2, 1)}
    near = jnp.stack([v, got[2], got[1], got[3]])
    return near, lax.ppermute(near, "brow", CORE)


def turned_sum(pieces, turns):
    got = [[lax.ppermute(p[k], "bcol", turn(k)) for p, turn in zip(pieces, turns)] for k in (2, 1, 3)]
    return [p[0].astype(F32) + ((g[0].astype(F32) + g[1].astype(F32)) + g[2].astype(F32))
            for p, g in zip(pieces, zip(*got))]


def two_phases(x_parts, p_parts):
    x, p = turned_sum([x_parts, p_parts], [x_turn, y_turn])
    x, p = x.astype(F32), p.astype(F32)
    x_own, p_own = x[0], p[0]
    x, p = x.astype(BF), p.astype(BF)
    x = [x_own] + [x[k] for k in (1, 2, 3)]
    p = [p_own] + [p[k] for k in (1, 2, 3)]
    return turned_sum([x, p], [y_turn, x_turn])


def sum_all(g):
    half = g.shape[0] // 2
    me = lax.axis_index("brow") % 2
    mine = lax.dynamic_slice_in_dim(g, me * half, half, 0)
    other = lax.dynamic_slice_in_dim(g, (1 - me) * half, half, 0)
    v = mine + lax.ppermute(other, "brow", CORE)
    for axis, turn in (("bcol", x_turn), ("brow", z_turn), ("bcol", y_turn)):
        a, b, c = [lax.ppermute(v, axis, turn(k)) for k in (2, 1, 3)]
        v = (v + a) + (b + c)
    return v, lax.ppermute(v, "brow", CORE)


def local(blocks, pattern_rows, pattern_cols, live_count, degree_scale, eigen_block, direction, cutoff):
    block_set = blocks[0, 0]
    wanted = eigen_block.shape[0]
    owners = lax.axis_size("bcol")
    brow = lax.axis_index("brow")
    sub = eigen_block.shape[1] // block_set.shape[-1]
    rows, source, live = pattern_rows[0, 0], pattern_cols[0, 0] // sub, live_count[0, 0]
    rows = jnp.where(jnp.arange(rows.shape[0]) < live, rows, owners * sub)
    turn = (brow // 2 - source // 2) % 4
    place = jnp.where(turn == 1, 2, jnp.where(turn == 2, 1, turn))
    spots = (place + 4 * ((brow - source) % 2)) * sub + pattern_cols[0, 0] % sub
    bcol = lax.axis_index("bcol")
    table = jnp.concatenate([rows, spots, jnp.stack([live, bcol // 4, bcol % 4])])

    def apply_graph(v, fetched=False):
        near, far = gather_brow((degree_scale * v).astype(BF))
        part = graph_partial(table, near, far, block_set, owners, fetched)
        got = lax.all_to_all(part, "bcol", 0, 0)
        return degree_scale * jnp.sum(got.astype(F32), axis=0)

    def apply_both(v, fetched=False):
        near, far = gather_brow((degree_scale * v).astype(BF))
        parts = graph_partial(table, near, far, block_set, owners, fetched, True)
        found = two_phases(parts[:4], parts[4:])
        return [degree_scale * f for f in found]

    x0, p0 = eigen_block, direction
    x1, p1 = apply_both(jnp.concatenate([x0, p0], 0), True)
    x2, p2 = apply_both(jnp.concatenate([x1, p1], 0))
    x3 = apply_graph(x2)
    parts = [x0, p0, x1, p1, x2, p2, x3]
    mine, other = sum_all(packed_gram(parts))
    return tuple(small(cutoff, (brow % 2).reshape(1), mine, other, parts))


def solution(mesh):
    docs = P(None, ("brow", "bcol"))
    return jax.shard_map(
        local,
        mesh=mesh,
        in_specs=(
            P("brow", "bcol", None, None, None),
            P("brow", "bcol", None),
            P("brow", "bcol", None),
            P("brow", "bcol"),
            P(("brow", "bcol")),
            docs,
            docs,
            P(),
        ),
        out_specs=(docs, docs, docs, docs),
        check_vma=False,
    )
```

```python
import functools

import jax
import jax.numpy as jnp
from jax import lax
from jax.experimental import pallas as pl
from jax.experimental.pallas import tpu as pltpu
from jax.sharding import PartitionSpec as P

ITERS = 2
NS_STEPS = 8
CHUNK = 8
HIGH = lax.Precision.HIGHEST
BF = jnp.bfloat16
F32 = jnp.float32
SMEM = pl.BlockSpec(memory_space=pltpu.SMEM)
VMEM = pl.BlockSpec(memory_space=pltpu.VMEM)


def nn(a, b):
    return lax.dot_general(a, b, (((1,), (0,)), ((), ())), precision=HIGH, preferred_element_type=F32)


def nt(a, b):
    return lax.dot_general(a, b, (((1,), (1,)), ((), ())), precision=HIGH, preferred_element_type=F32)


def graph_kernel(n_out, table_ref, near_ref, far_ref, blocks_ref, *rest):
    outs, (panel, acc, *own) = rest[:n_out], rest[n_out:]
    n_slots = blocks_ref.shape[0]
    live = table_ref[2 * n_slots]
    sub = panel.shape[0] // 8
    chunks = n_slots // CHUNK
    held = own[0] if own else blocks_ref

    def fetch(c):
        part = pl.ds(c * CHUNK, CHUNK)
        return pltpu.make_async_copy(blocks_ref.at[part], held.at[part], own[1].at[c])

    for c in range(chunks if own else 0):
        @pl.when(c * CHUNK < live)
        def _():
            fetch(c).start()

    for s in range(8):
        src = near_ref if s < 4 else far_ref
        for q in range(sub):
            panel[s * sub + q] = src[s % 4, :, q * 256:(q + 1) * 256]
    acc[...] = jnp.zeros_like(acc)

    for c in range(chunks):
        @pl.when(c * CHUNK < live)
        def _():
            if own:
                fetch(c).wait()
            slots = range(c * CHUNK, (c + 1) * CHUNK)
            prods = [lax.dot_general(panel[table_ref[n_slots + s]], held[s], (((1,), (1,)), ((), ())),
                                     preferred_element_type=F32) for s in slots]
            for s, prod in zip(slots, prods):
                row = table_ref[s]
                acc[row] = acc[row] + prod
    if n_out == 1:
        out_ref = outs[0]
        for j in range(out_ref.shape[0]):
            for q in range(sub):
                out_ref[j, :, q * 256:(q + 1) * 256] = acc[j * sub + q].astype(BF)
        return
    mx, my = table_ref[2 * n_slots + 1], table_ref[2 * n_slots + 2]
    half = acc.shape[1] // 2
    for k in range(4):
        for m in range(4):
            for_x = jnp.bitwise_and(mx + k, 3) * 4 + jnp.bitwise_and(my + m, 3)
            for_p = jnp.bitwise_and(mx + m, 3) * 4 + jnp.bitwise_and(my + k, 3)
            for q in range(sub):
                columns = pl.ds(q * 256, 256)
                outs[k][m, :, columns] = acc[for_x * sub + q, :half].astype(BF)
                outs[4 + k][m, :, columns] = acc[for_p * sub + q, half:].astype(BF)


def graph_partial(table, near, far, blocks, owners, fetched, split=False):
    n_slots, side, _ = blocks.shape
    r, width = near.shape[1:]
    sub = width // side
    own = [pltpu.VMEM((n_slots, side, side), BF), pltpu.SemaphoreType.DMA((n_slots // CHUNK,))]
    return pl.pallas_call(
        functools.partial(graph_kernel, 8 if split else 1),
        out_shape=([jax.ShapeDtypeStruct((4, r // 2, width), BF)] * 8 if split
                   else jax.ShapeDtypeStruct((owners, r, width), BF)),
        in_specs=[SMEM] + [VMEM] * 2 + [pl.BlockSpec(memory_space=pltpu.HBM) if fetched else VMEM],
        out_specs=[VMEM] * 8 if split else VMEM,
        scratch_shapes=[
            pltpu.VMEM((8 * sub, r, side), BF),
            pltpu.VMEM((owners * sub + 1, r, side), F32),
        ] + (own if fetched else []),
        compiler_params=pltpu.CompilerParams(vmem_limit_bytes=(50 if fetched else 14) * 2**20),
        name="graph_partial",
    )(table, near, far, blocks)


def halves(a):
    top = a.astype(BF)
    return top, (a - top.astype(F32)).astype(BF)


def three(a, b):
    ah, al = halves(a)
    bh, bl = halves(b)

    def dot(u, v):
        return lax.dot_general(u, v, (((1,), (0,)), ((), ())), preferred_element_type=F32)

    return dot(ah, bh) + (dot(ah, bl) + dot(al, bh))


def eye_mask(n):
    return (lax.broadcasted_iota(jnp.int32, (n, n), 0) == lax.broadcasted_iota(jnp.int32, (n, n), 1))


def sweep_inverse(ref):
    n = ref.shape[0]
    ri = lax.broadcasted_iota(jnp.int32, (n, n), 0)
    ci = lax.broadcasted_iota(jnp.int32, (n, n), 1)

    def step(k, carry):
        a = ref[...]
        col = jnp.sum(jnp.where(ci == k, a, 0.0), axis=1, keepdims=True)
        row = jnp.sum(jnp.where(ri == k, a, 0.0), axis=0, keepdims=True)
        pivot = jnp.sum(jnp.where(ci[:1] == k, row, 0.0), axis=1, keepdims=True)
        col = jnp.where(ri[:, :1] == k, -1.0, col)
        row = jnp.where(ci[:1] == k, -1.0, row) / pivot
        ref[...] = jnp.where((ri == k) | (ci == k), 0.0, a) - col * row
        return carry

    lax.fori_loop(0, n, step, 0)
    ref[...] = -ref[...]


def square_sum(a):
    return jnp.sum(a * a)


def spd_inverses(mats, refs):
    scaled, lefts, rights, errs, sums = [], [], [], [], []
    for a in mats:
        eye = eye_mask(a.shape[0])
        diag = jnp.where(eye, a, 0.0)
        left = lax.rsqrt(jnp.sum(diag, axis=1, keepdims=True))
        right = lax.rsqrt(jnp.sum(diag, axis=0, keepdims=True))
        a = a * left * right
        rows = jnp.sum(jnp.abs(a), axis=0, keepdims=True)
        inv = 1.0 / jnp.max(rows, axis=1, keepdims=True)
        unit = eye.astype(F32)
        err = unit - a * inv
        scaled.append(a)
        lefts.append(left)
        rights.append(right)
        errs.append(err)
        sums.append((unit + err) * inv)

    def levels(errs, sums, count):
        for _ in range(count):
            errs = [nn(e, e) for e in errs]
            sums = [s + nn(s, e) for s, e in zip(sums, errs)]
        for (err_ref, sum_ref), e, s in zip(refs, errs, sums):
            err_ref[...] = e
            sum_ref[...] = s
        return sum(square_sum(e) for e in errs)

    def body(state):
        level, _ = state
        size = levels([r[0][...] for r in refs], [r[1][...] for r in refs], 1)
        return level + 1, size

    size = levels(errs, sums, 4)
    _, size = lax.while_loop(lambda s: (s[1] > 1e-8) & (s[0] < 24), body, (jnp.int32(0), size))
    good = size <= 1e-8

    @pl.when(jnp.logical_not(good))
    def _():
        for a, (_, sum_ref) in zip(scaled, refs):
            sum_ref[...] = a
            sweep_inverse(sum_ref)

    return [left * r[1][...] * right for left, right, r in zip(lefts, rights, refs)]


def sign_rows(sym, inverse, cutoff, wanted):
    eye = eye_mask(sym.shape[0]).astype(F32)
    s = (cutoff - 1.0) * eye + nn(sym, inverse)
    s2 = nn(s, s)
    total = jnp.sum(jnp.sum(s2 * eye, axis=1, keepdims=True), axis=0, keepdims=True)
    scale = lax.rsqrt(total + 1e-06)
    s = s * scale
    s2 = s2 * (scale * scale)
    s = 1.5 * s - 0.5 * three(s, s2)
    for _ in range(NS_STEPS - 1):
        s = 1.5 * s - 0.5 * three(s, three(s, s))
    return 0.5 * (eye + s)[:wanted]


def shift(v, wanted):
    return pltpu.roll(v, 2 * wanted, 1)


def fill_gram(packed, full, w):
    full[...] = jnp.zeros_like(full)

    def put(i, j, block):
        full[i * w:(i + 1) * w, j * w:(j + 1) * w] = block
        if i != j:
            full[j * w:(j + 1) * w, i * w:(i + 1) * w] = block.T

    for row, i in enumerate((0, 4, 5, 6)):
        for j in range(4):
            put(i, j, packed[row * w:(row + 1) * w, j * w:(j + 1) * w])
    for row, spots in ((4, ((1, 1), (1, 2), (1, 3), (4, 4))), (5, ((2, 2), (2, 3), (3, 3), (5, 4)))):
        for place, (i, j) in enumerate(spots):
            put(i, j, packed[row * w:(row + 1) * w, place * w:(place + 1) * w])
    q = w // 4
    put(6, 4, jnp.concatenate([packed[6 * w:6 * w + q, n * w:(n + 1) * w] for n in range(4)], 0))


def next_block(rows, basis, gram, inverse_x, width, w):
    zt = nn(gram[2 * w:, :w], inverse_x)
    both = jnp.concatenate([rows, jnp.concatenate([-nn(rows[:, 2 * w:], zt), rows[:, w:]], 1)], 0)
    if basis is None:
        both = jnp.concatenate([both, jnp.zeros((2 * w, width - 3 * w), F32)], 1)
    else:
        both = nn(both, basis)
    return both[:w], both[w:]


def small_kernel(w, cut_ref, core_ref, mine_ref, other_ref, *rest):
    parts, outs, (full, e96, s96, e32, s32) = rest[:7], rest[7:11], rest[11:]
    refs = [(e96, s96), (e32, s32)]
    mine, other = mine_ref[...], other_ref[...]
    first = core_ref[0] == 0
    fill_gram(jnp.concatenate([jnp.where(first, mine, other), jnp.where(first, other, mine)], 0), full, w)
    width = full.shape[0]
    gram = full[:3 * w, :3 * w]
    sym = 0.5 * (full[:3 * w, 2 * w:5 * w] + full[2 * w:5 * w, :3 * w])
    basis = None
    for _ in range(ITERS - 1):
        inverse, inverse_x = spd_inverses([gram, gram[:w, :w]], refs)
        rows = sign_rows(sym, inverse, cut_ref[0], w)
        x, p = next_block(rows, basis, gram, inverse_x, width, w)
        basis = jnp.concatenate([x, p, shift(x, w)], 0)
        tb = nn(basis, full[...])
        moved = shift(basis, w)
        gram = nt(tb, basis)
        sym = 0.5 * (nt(tb, moved) + nt(moved, tb))
    inverse, inverse_x = spd_inverses([gram, gram[:w, :w]], refs)
    rows = sign_rows(sym, inverse, cut_ref[0], w)
    x, p = next_block(rows, basis, gram, inverse_x, width, w)
    tx = nn(rows, tb)
    moved = shift(x, w)
    (inverse_x,) = spd_inverses([nt(tx, x)], refs[1:])
    zt = nn(nt(moved, tx), inverse_x)
    coeffs = jnp.concatenate([x, p, nn(zt, x) - moved, p - shift(p, w)], 0)
    krylov = jnp.concatenate([r[...] for r in parts] + [jnp.zeros_like(parts[0])], 0)
    found = nn(coeffs, krylov)
    for n, out_ref in enumerate(outs):
        out_ref[...] = found[n * w:(n + 1) * w]


def small(cutoff, core, mine, other, parts):
    w = parts[0].shape[0]
    return pl.pallas_call(
        functools.partial(small_kernel, w),
        out_shape=[jax.ShapeDtypeStruct(parts[0].shape, F32)] * 4,
        in_specs=[SMEM, SMEM] + [VMEM] * 9,
        out_specs=[VMEM] * 4,
        scratch_shapes=[pltpu.VMEM((n, n), F32) for n in (8 * w, 3 * w, 3 * w, w, w)],
        compiler_params=pltpu.CompilerParams(vmem_limit_bytes=16 * 2**20),
        name="small_matrices",
    )(cutoff, core, mine, other, *parts)


def gram_kernel(*refs):
    k = [r[...] for r in refs[:-1]]
    out_ref = refs[-1]
    w = k[0].shape[0]
    out_ref[:3 * w] = nt(jnp.concatenate([k[0], k[4], k[5]], 0), jnp.concatenate(k[:4], 0))
    inner = jnp.concatenate(k[1:4], 0)
    inner = nt(inner, inner)
    outer = nt(jnp.concatenate(k[4:], 0), k[4])
    out_ref[3 * w:4 * w] = jnp.concatenate([inner[:w], outer[:w]], 1)
    out_ref[4 * w:] = jnp.concatenate([inner[w:2 * w, w:], inner[2 * w:, 2 * w:], outer[w:]], 1)


def last_gram_kernel(*refs):
    k = [r[...] for r in refs[:6]]
    found_ref, out_ref = refs[6:]
    w = k[0].shape[0]
    last = nt(k[5], jnp.concatenate(k[:5], 0))
    out_ref[:3 * w] = found_ref[:3 * w]
    out_ref[3 * w:4 * w] = last[:, :4 * w]
    out_ref[4 * w:6 * w] = found_ref[3 * w:]
    q = w // 4
    out_ref[6 * w:6 * w + q] = jnp.concatenate([last[n * q:(n + 1) * q, 4 * w:] for n in range(4)], 1)
    out_ref[6 * w + q:] = jnp.zeros_like(out_ref[6 * w + q:])


def gram_call(kernel, name, rows, *arrays):
    return pl.pallas_call(
        kernel,
        out_shape=jax.ShapeDtypeStruct((rows, 4 * arrays[0].shape[0]), F32),
        in_specs=[VMEM] * len(arrays),
        out_specs=VMEM,
        compiler_params=pltpu.CompilerParams(vmem_limit_bytes=16 * 2**20),
        name=name,
    )(*arrays)


def packed_gram(blocks):
    w = blocks[0].shape[0]
    found = gram_call(gram_kernel, "first_gram", 5 * w, *blocks[:6])
    return gram_call(last_gram_kernel, "packed_gram", 6 * w + w // 2, *blocks[:5], blocks[6], found)


def z_turn(k):
    return [(i, (i + 2 * k) % 8) for i in range(8)]


def y_turn(k):
    return [(i, (i // 4) * 4 + (i + k) % 4) for i in range(16)]


def x_turn(k):
    return [(i, (i + 4 * k) % 16) for i in range(16)]


CORE = [(i, i ^ 1) for i in range(8)]


def gather_brow(v):
    got = {k: lax.ppermute(v, "brow", z_turn(k)) for k in (3, 2, 1)}
    near = jnp.stack([v, got[2], got[1], got[3]])
    return near, lax.ppermute(near, "brow", CORE)


def turned_sum(pieces, turns):
    got = [[lax.ppermute(p[k], "bcol", turn(k)) for p, turn in zip(pieces, turns)] for k in (2, 1, 3)]
    return [p[0].astype(F32) + ((g[0].astype(F32) + g[1].astype(F32)) + g[2].astype(F32))
            for p, g in zip(pieces, zip(*got))]


def two_phases(x_parts, p_parts):
    x, p = turned_sum([x_parts, p_parts], [x_turn, y_turn])
    x, p = x.astype(F32), p.astype(F32)
    x_own, p_own = x[0], p[0]
    x, p = x.astype(BF), p.astype(BF)
    x = [x_own] + [x[k] for k in (1, 2, 3)]
    p = [p_own] + [p[k] for k in (1, 2, 3)]
    return turned_sum([x], [y_turn])[0], p


def kept_kernel(v_ref, after_ref, out_ref):
    out_ref[...] = v_ref[...]


def late_phase(p, after):
    sent = jnp.stack(p[1:])
    sent = pl.pallas_call(
        kept_kernel,
        out_shape=jax.ShapeDtypeStruct(sent.shape, BF),
        in_specs=[VMEM, pl.BlockSpec(memory_space=pl.ANY)],
        out_specs=VMEM,
        compiler_params=pltpu.CompilerParams(vmem_limit_bytes=8 * 2**20),
        name="kept_pieces",
    )(sent, after)
    return turned_sum([[p[0], sent[0], sent[1], sent[2]]], [x_turn])[0]


def sum_all(g):
    half = g.shape[0] // 2
    me = lax.axis_index("brow") % 2
    mine = lax.dynamic_slice_in_dim(g, me * half, half, 0)
    other = lax.dynamic_slice_in_dim(g, (1 - me) * half, half, 0)
    v = mine + lax.ppermute(other, "brow", CORE)
    for axis, turn in (("bcol", x_turn), ("brow", z_turn), ("bcol", y_turn)):
        a, b, c = [lax.ppermute(v, axis, turn(k)) for k in (2, 1, 3)]
        v = (v + a) + (b + c)
    return v, lax.ppermute(v, "brow", CORE)


def local(blocks, pattern_rows, pattern_cols, live_count, degree_scale, eigen_block, direction, cutoff):
    block_set = blocks[0, 0]
    wanted = eigen_block.shape[0]
    owners = lax.axis_size("bcol")
    brow = lax.axis_index("brow")
    sub = eigen_block.shape[1] // block_set.shape[-1]
    rows, source, live = pattern_rows[0, 0], pattern_cols[0, 0] // sub, live_count[0, 0]
    rows = jnp.where(jnp.arange(rows.shape[0]) < live, rows, owners * sub)
    turn = (brow // 2 - source // 2) % 4
    place = jnp.where(turn == 1, 2, jnp.where(turn == 2, 1, turn))
    spots = (place + 4 * ((brow - source) % 2)) * sub + pattern_cols[0, 0] % sub
    bcol = lax.axis_index("bcol")
    table = jnp.concatenate([rows, spots, jnp.stack([live, bcol // 4, bcol % 4])])

    def apply_both(v, fetched=False):
        near, far = gather_brow((degree_scale * v).astype(BF))
        parts = graph_partial(table, near, far, block_set, owners, fetched, True)
        found, p = two_phases(parts[:4], parts[4:])
        return degree_scale * found, p

    x0, p0 = eigen_block, direction
    x1, p1 = apply_both(jnp.concatenate([x0, p0], 0), True)
    p1 = degree_scale * turned_sum([p1], [x_turn])[0]
    x2, p2 = apply_both(jnp.concatenate([x1, p1], 0))
    near, far = gather_brow((degree_scale * x2).astype(BF))
    part = graph_partial(table, near, far, block_set, owners, False)
    p2 = degree_scale * late_phase(p2, part)
    x3 = degree_scale * jnp.sum(lax.all_to_all(part, "bcol", 0, 0).astype(F32), axis=0)
    parts = [x0, p0, x1, p1, x2, p2, x3]
    mine, other = sum_all(packed_gram(parts))
    return tuple(small(cutoff, (brow % 2).reshape(1), mine, other, parts))


def solution(mesh):
    docs = P(None, ("brow", "bcol"))
    return jax.shard_map(
        local,
        mesh=mesh,
        in_specs=(
            P("brow", "bcol", None, None, None),
            P("brow", "bcol", None),
            P("brow", "bcol", None),
            P("brow", "bcol"),
            P(("brow", "bcol")),
            docs,
            docs,
            P(),
        ),
        out_specs=(docs, docs, docs, docs),
        check_vma=False,
    )
```
